512 devices in a mesh: section: 8 (over x, z_hi), ctx: 64 (over y, z_lo, core).
Axes of the slice: x: 4, y: 8, z: 8 (z_hi: 2, z_lo: 4; z = z_hi * 4 + z_lo), core: 2. Of those that a mesh axis runs over, the one named last changes fastest.
Arguments:
- section_in: bfloat16 [8, 8192, 4096], P('section', 'ctx'), may hold values from -12 to 12
- back_in: bfloat16 [8, 8192, 4096], P('section', 'ctx'), may hold values from -12 to 12
- upstream: bfloat16 [8, 8192, 4096], P('section', 'ctx'), may hold values from -6 to 6
- gains: float32 [8, 4096], P('section'), may hold values from 0.25 to 1.75
- kv_weight: bfloat16 [8, 4096, 1024], P('section', 'ctx')
Outputs:
- next_in: bfloat16 [8, 8192, 4096], P('section', 'ctx')
- next_grad: bfloat16 [8, 8192, 4096], P('section', 'ctx')
- gain_grad: float32 [8, 4096], P('section')
The draws below stay inside these ranges and needn't reach their ends.
All inputs are finite; a program needn't handle non-finite values.
Results may differ from the reference program's by a relative error of at most 0.012.
Values may be sent and summed in bfloat16 or wider, within the bound.
No kernel may reach another device: no remote copies, remote signals or barrier semaphores. Data moves between devices by JAX's collectives and lax.ppermute only.
A program may use at most 64 MiB of HBM per device.

```python
import jax
import jax.numpy as jnp
from jax import lax

KV_HEADS = 4
HD = 128
STEPS = 2
TOK_DEV = 128
W = 4096
KVW = 512
GROUP = 8
SEQ = 8192
N_SECTION = 8
N_CTX = 64


def draw_section_in(key, part):
    key = jax.random.fold_in(key, 11)
    base_rows = jnp.clip(jax.random.normal(jax.random.fold_in(key, 1), (N_SECTION, SEQ, W), jnp.float32), -6.0, 6.0)
    return base_rows.astype(jnp.bfloat16)


def draw_back_in(key, part):
    key = jax.random.fold_in(key, 13)
    base_rows = jnp.clip(jax.random.normal(jax.random.fold_in(key, 1), (N_SECTION, SEQ, W), jnp.float32), -6.0, 6.0)
    return base_rows.astype(jnp.bfloat16)


def draw_kv_weight(key, part):
    key = jax.random.fold_in(key, 23)
    weights = jnp.clip(jax.random.normal(key, (N_SECTION, W, 2 * KVW), jnp.float32), -6.0, 6.0) * W ** (-0.5)
    return weights.astype(jnp.bfloat16)


def levels(key, extent, split, low, top_value):
    loudness = 1.0
    for dim, parts in split:
        draws = jax.random.uniform(jax.random.fold_in(jax.random.fold_in(key, 6), dim), (parts,), jnp.float32, low / len(split), top_value / len(split))
        loudness = loudness * jnp.repeat(jnp.exp(draws), extent[dim] // parts).reshape((-1,) + (1,) * (len(extent) - 1 - dim))
    return loudness


def bell_draw(stream_key, extent, width, limit, shards=(), kind=jnp.bfloat16):
    result = width * jax.random.normal(stream_key, extent, jnp.float32)
    if shards:
        result = result * levels(stream_key, extent, shards, -0.22, 0.18)
    return jnp.clip(result, -limit, limit).astype(kind)


def setup_inputs(seed: int = 0) -> dict:
    arg_keys = jax.random.split(jax.random.key(seed), 6)
    return {
        "section_in": draw_section_in(jax.random.fold_in(arg_keys[5], 71), 0),
        "back_in": draw_back_in(jax.random.fold_in(arg_keys[5], 71), 0),
        "upstream": bell_draw(arg_keys[2], (N_SECTION, SEQ, W), 1.0, 6.0, ((0, 8), (1, 64))),
        "gains": jnp.clip(1.0 + 0.15 * jax.random.normal(arg_keys[3], (N_SECTION, W), jnp.float32), 0.25, 1.75),
        "kv_weight": draw_kv_weight(jax.random.fold_in(arg_keys[5], 71), 0),
    }


EPSILON = 1e-05

def norm_forward(section_x, gain_row):
    values = section_x.astype(jnp.float32)
    inv_rms = lax.rsqrt(lax.optimization_barrier(jnp.mean(values * values, axis=-1, keepdims=True)) + EPSILON)
    scaled = values * inv_rms
    return (scaled, inv_rms, (scaled * gain_row).astype(jnp.bfloat16))

def key_mask(block_id):
    span = (STEPS + 1) * TOK_DEV
    tok_pos = jnp.arange(TOK_DEV, dtype=jnp.int32)[:, None]
    slot_pos = jnp.arange(span, dtype=jnp.int32)[None, :]
    slot_block = slot_pos // TOK_DEV
    earlier = slot_block < STEPS
    present = block_id - STEPS + slot_block >= 0
    causal = slot_pos - slot_block * TOK_DEV <= tok_pos
    return present & (earlier | causal)

def block_probs(queries, keys, key_valid):
    score_scale = HD ** (-0.5)
    logits = jnp.einsum('tkgd,lkd->kgtl', queries.astype(jnp.float32), keys.astype(jnp.float32)) * score_scale
    logits = jnp.where(key_valid, logits, -1e+30)
    row_max = lax.optimization_barrier(jnp.max(logits, axis=-1, keepdims=True))
    exp_terms = jnp.exp(logits - row_max)
    probs = exp_terms / lax.optimization_barrier(jnp.sum(exp_terms, axis=-1, keepdims=True))
    return (probs, probs.astype(jnp.bfloat16))

def window_of(padded_kv, block_id):
    span = (STEPS + 1) * TOK_DEV
    window_kv = lax.dynamic_slice_in_dim(padded_kv, (block_id * TOK_DEV).astype(jnp.int32), span, 0)
    keys = window_kv[:, :KVW].reshape(span, KV_HEADS, HD)
    values = window_kv[:, KVW:].reshape(span, KV_HEADS, HD)
    return (keys, values)

def layer_forward(section_x, gain_row, weight):
    block_ids = jnp.arange(N_CTX, dtype=jnp.int32)
    scaled, inv_rms, normed = norm_forward(section_x, gain_row)
    key_values = jnp.dot(normed, weight, preferred_element_type=jnp.float32).astype(jnp.bfloat16)
    padded_kv = jnp.concatenate([jnp.zeros((STEPS * TOK_DEV, 2 * KVW), jnp.bfloat16), key_values], axis=0)

    def attend_block(block_id):
        queries = lax.dynamic_slice_in_dim(normed, (block_id * TOK_DEV).astype(jnp.int32), TOK_DEV, 0)
        queries = queries.reshape(TOK_DEV, KV_HEADS, GROUP, HD)
        keys, values = window_of(padded_kv, block_id)
        probs, probs_b = block_probs(queries, keys, key_mask(block_id))
        attended = jnp.einsum('kgtl,lkd->tkgd', probs_b.astype(jnp.float32), values.astype(jnp.float32))
        return attended.reshape(TOK_DEV, W)
    attended = lax.map(attend_block, block_ids).reshape(SEQ, W)
    layer_out = (section_x.astype(jnp.float32) + attended).astype(jnp.bfloat16)
    return (layer_out, (scaled, inv_rms, normed, padded_kv, attended))

def layer_backward(upper_in, saved, gain_row, weight):
    scaled, inv_rms, normed, padded_kv, attended = saved
    span = (STEPS + 1) * TOK_DEV
    block_ids = jnp.arange(N_CTX, dtype=jnp.int32)
    score_scale = HD ** (-0.5)

    def back_block(running, block_id):
        start = (block_id * TOK_DEV).astype(jnp.int32)
        queries = lax.dynamic_slice_in_dim(normed, start, TOK_DEV, 0).reshape(TOK_DEV, KV_HEADS, GROUP, HD)
        upper = lax.dynamic_slice_in_dim(upper_in, start, TOK_DEV, 0).reshape(TOK_DEV, KV_HEADS, GROUP, HD)
        block_out = lax.dynamic_slice_in_dim(attended, start, TOK_DEV, 0).reshape(TOK_DEV, KV_HEADS, GROUP, HD)
        keys, values = window_of(padded_kv, block_id)
        probs, probs_b = block_probs(queries, keys, key_mask(block_id))
        upper32 = upper.astype(jnp.float32)
        grad_probs = jnp.einsum('tkgd,lkd->kgtl', upper32, values.astype(jnp.float32))
        row_dot = jnp.einsum('tkgd,tkgd->kgt', upper32, block_out)
        dlogits = (probs * (grad_probs - row_dot[..., None]) * score_scale).astype(jnp.bfloat16)
        dlogits32 = dlogits.astype(jnp.float32)
        grad_query = jnp.einsum('kgtl,lkd->tkgd', dlogits32, keys.astype(jnp.float32))
        grad_keys = jnp.einsum('kgtl,tkgd->lkd', dlogits32, queries.astype(jnp.float32))
        grad_values = jnp.einsum('kgtl,tkgd->lkd', probs_b.astype(jnp.float32), upper32)
        piece = jnp.concatenate([grad_keys.reshape(span, KVW), grad_values.reshape(span, KVW)], axis=1)
        current = lax.dynamic_slice_in_dim(running, start, span, 0)
        running = lax.dynamic_update_slice_in_dim(running, current + piece, start, 0)
        return (running, grad_query.reshape(TOK_DEV, W))
    start_carry = jnp.zeros(((N_CTX + STEPS) * TOK_DEV, 2 * KVW), jnp.float32)
    grad_padded, grad_query = lax.scan(back_block, start_carry, block_ids)
    grad_kv = grad_padded[STEPS * TOK_DEV:].astype(jnp.bfloat16)
    grad_normed = grad_query.reshape(SEQ, W) + jnp.dot(grad_kv, weight.T, preferred_element_type=jnp.float32)
    gain_grad = lax.optimization_barrier(jnp.sum(grad_normed * scaled, axis=0))
    grad_scaled = grad_normed * gain_row
    inner = lax.optimization_barrier(jnp.mean(grad_scaled * scaled, axis=-1, keepdims=True))
    grad_input = inv_rms * (grad_scaled - scaled * inner) + upper_in.astype(jnp.float32)
    return (grad_input.astype(jnp.bfloat16), gain_grad)

def reference(section_in, back_in, upstream, gains, kv_weight):
    outputs = []
    grads = []
    gain_grads = []
    for layer in range(N_SECTION):
        layer_out, unused = layer_forward(section_in[layer], gains[layer], kv_weight[layer])
        outputs.append(layer_out)
        recomputed, saved = layer_forward(back_in[layer], gains[layer], kv_weight[layer])
        grad_input, gain_grad = layer_backward(upstream[layer], saved, gains[layer], kv_weight[layer])
        grads.append(grad_input)
        gain_grads.append(gain_grad)
    next_in = jnp.roll(jnp.stack(outputs), 1, axis=0)
    next_grad = jnp.roll(jnp.stack(grads), -1, axis=0)
    return (next_in, next_grad, jnp.stack(gain_grads))
```

```python
import functools

import jax
import jax.numpy as jnp
from jax import lax
from jax.experimental import pallas as pl
from jax.experimental.pallas import tpu as pltpu
from jax.sharding import PartitionSpec as P

HD = 128
STEPS = 2
EPSILON = 1e-05
GROUP = 8
KVH = 4
TOK = 128
SPAN = (STEPS + 1) * TOK

X, Z_HI, Y, Z_LO, CORES = 4, 2, 8, 4, 2
Z = Z_HI * Z_LO
CTX = Y * Z_LO * CORES

SCALE = HD ** (-0.5)
LOG2E = 1.4426950408889634


def ctx_pairs(move):
    pairs = []
    for c in range(CTX):
        target = move(c // (Z_LO * CORES), (c // CORES) % Z_LO, c % CORES)
        if target is not None:
            y, z_lo, core = target
            pairs.append((c, (y * Z_LO + z_lo) * CORES + core))
    return pairs


def over_ctx(value, move):
    return lax.ppermute(value, "ctx", ctx_pairs(move))


def grid_pairs(move):
    pairs = []
    for x in range(X):
        for z in range(Z):
            new_x, new_z = move(x, z)
            new_x, new_z = (new_x % X, new_z % Z)
            for y in range(Y):
                for core in range(CORES):
                    source = (x * Z_HI + z // Z_LO) * CTX + (y * Z_LO + z % Z_LO) * CORES + core
                    target = (new_x * Z_HI + new_z // Z_LO) * CTX + (y * Z_LO + new_z % Z_LO) * CORES + core
                    pairs.append((source, target))
    return pairs


def over_grid(value, move):
    return lax.ppermute(value, ("section", "ctx"), grid_pairs(move))


def halfway(value, way):
    return over_grid(value, lambda x, z: (x, z + 2 * way))


def arrive(value, way, distance):
    def move(x, z):
        z_hi = ((z - 2 * way) % Z) // Z_LO
        cross = (1 if z_hi == Z_HI - 1 else 0) if distance == 1 else (-1 if z_hi == 0 else 0)
        return (x + cross, z + 2 * way)

    return over_grid(value, move)


def set_out(upper, lower):
    return halfway(upper, 1), halfway(lower, -1)


def land(halves, distance):
    return arrive(halves[0], 1, distance), arrive(halves[1], -1, distance)


def norm_forward(section_x, gain_row):
    values = section_x.astype(jnp.float32)
    inv_rms = lax.rsqrt(jnp.mean(values * values, axis=-1, keepdims=True) + EPSILON)
    return (values * inv_rms * gain_row).astype(jnp.bfloat16)


def by_head(kv_columns):
    parts = []
    for head in range(KVH):
        parts.append(kv_columns[:, head * HD : (head + 1) * HD])
        parts.append(kv_columns[:, (KVH + head) * HD : (KVH + head + 1) * HD])
    return jnp.concatenate(parts, axis=1)


def gather_weight(own_rows, core, z_lo, y, start_crossing):
    half = own_rows.shape[1] // 2
    columns = by_head(own_rows)
    low, high = columns[:, :half], columns[:, half:]
    keep = jnp.where(core == 0, low, high)
    received = over_ctx(jnp.where(core == 0, high, low), lambda y, z, c: (y, z, 1 - c))
    chip = jnp.concatenate(
        [jnp.where(core == 0, keep, received), jnp.where(core == 0, received, keep)], axis=0
    )
    rows = chip.shape[0]
    pieces = [chip]
    for step in range(1, Z_LO):
        pieces.append(over_ctx(chip, lambda y, z, c, step=step: (y, (z + step) % Z_LO, c)))
    back = pieces[::-1]
    run = lax.dynamic_slice_in_dim(
        jnp.concatenate(back + back[:-1], axis=0), (Z_LO - 1 - z_lo) * rows, Z_LO * rows, 0
    )
    block = Z_LO * rows
    weight = jnp.zeros((Y * block, half), own_rows.dtype)

    def place(weight, piece, at, offset=0):
        return lax.dynamic_update_slice_in_dim(weight, piece, (at % Y) * block + offset, 0)

    def up(piece):
        return over_ctx(piece, lambda y, z, c: ((y + 1) % Y, z, c))

    def down(piece):
        return over_ctx(piece, lambda y, z, c: ((y - 1) % Y, z, c))

    weight = place(weight, run, y)
    rising, falling = run, run
    for step in range(1, Y // 2):
        rising, falling = up(rising), down(falling)
        weight = place(weight, rising, y - step + Y)
        weight = place(weight, falling, y + step)
        if step == 1:
            crossing = start_crossing(run)
        if step == 3:
            (rising, falling), crossing = lax.optimization_barrier(((rising, falling), crossing))
    last_rising, last_falling = up(rising[: block // 2]), down(falling[block // 2 :])
    weight = place(weight, last_rising, y + Y // 2)
    weight = place(weight, last_falling, y + Y // 2, block // 2)
    return weight, crossing


def swap(value):
    return over_ctx(value, lambda y, z, c: (y, z, 1 - c))


def chip_rows(own, partner, core):
    return jnp.concatenate(
        [jnp.where(core == 0, own, partner), jnp.where(core == 0, partner, own)], axis=0
    )


def next_chip(y, z):
    chip = y * Z_LO + z + 1
    return None if chip == Y * Z_LO else (chip // Z_LO, chip % Z_LO)


def to_next(cross):
    def move(y, z, core):
        after = next_chip(y, z)
        return None if after is None else (after[0], after[1], core ^ cross)

    return move


def window(mine, core):
    other = swap(mine)
    same = over_ctx(mine, to_next(0))
    cross = over_ctx(mine, to_next(1))
    rows = jnp.concatenate([same, mine], axis=0)
    others = jnp.concatenate([cross, other], axis=0)
    return jnp.concatenate(
        [jnp.where(core == 0, rows, others), jnp.where(core == 0, others, rows)], axis=1
    )


def stacked(ref, first, count):
    return jnp.concatenate(
        [ref[:, (first + g) * HD : (first + g + 1) * HD] for g in range(count)], axis=0
    )


def masked_scores(keys, queries, block_id):
    scores = lax.dot_general(
        keys, queries, (((1,), (1,)), ((), ())), preferred_element_type=jnp.float32
    )
    across = queries.shape[0]
    parts = []
    for slot in range(STEPS):
        part = scores[slot * TOK : (slot + 1) * TOK]
        parts.append(jnp.where(block_id - STEPS + slot >= 0, part, -1e30))
    seen = lax.broadcasted_iota(jnp.int32, (TOK, across), 0)
    query = lax.broadcasted_iota(jnp.int32, (TOK, across), 1) % TOK
    parts.append(jnp.where(seen <= query, scores[STEPS * TOK :], -1e30))
    return jnp.concatenate(parts, axis=0)


PAIR = 2


def forward_kernel(block_ref, normed_ref, x_ref, kv_ref, out_ref):
    block_id = block_ref[0]
    first = pl.multiple_of((block_id % CORES) * TOK, TOK)
    kv = kv_ref[pl.ds(first, SPAN), :]
    keys, values = kv[:, :HD], kv[:, HD:]
    values_t = values.astype(jnp.float32).T.astype(jnp.bfloat16)
    for pair in range(GROUP // PAIR):
        queries = stacked(normed_ref, pair * PAIR, PAIR)
        scores = masked_scores(keys, queries, block_id)
        top = jnp.max(scores, axis=0, keepdims=True)
        terms = jnp.exp2((scores - top) * (SCALE * LOG2E))
        total = jnp.sum(terms, axis=0, keepdims=True)
        attended = jnp.dot(
            values_t, terms.astype(jnp.bfloat16), preferred_element_type=jnp.float32
        ) * (1.0 / total)
        for g in range(PAIR):
            at = (pair * PAIR + g) * HD
            out = attended[:, g * TOK : (g + 1) * TOK].T + x_ref[:, at : at + HD].astype(jnp.float32)
            out_ref[:, at : at + HD] = out.astype(jnp.bfloat16)


def forward_attention(block_id, normed, x, kv):
    wide = GROUP * HD
    return pl.pallas_call(
        forward_kernel,
        grid=(KVH,),
        in_specs=[
            pl.BlockSpec(memory_space=pltpu.SMEM),
            pl.BlockSpec((TOK, wide), lambda h: (0, h)),
            pl.BlockSpec((TOK, wide), lambda h: (0, h)),
            pl.BlockSpec((4 * TOK, 2 * HD), lambda h: (0, h)),
        ],
        out_specs=pl.BlockSpec((TOK, wide), lambda h: (0, h)),
        out_shape=jax.ShapeDtypeStruct(x.shape, jnp.bfloat16),
        compiler_params=pltpu.CompilerParams(vmem_limit_bytes=32 * 2**20),
        cost_estimate=pl.CostEstimate(
            flops=16 * 10**8, bytes_accessed=4 * 2**20, transcendentals=2 * 10**6
        ),
        name="forward_attention",
    )(block_id, normed, x, kv)


def backward_kernel(
    block_ref, normed_ref, upper_ref, kv_ref, dq_ref, far_ref, near_ref, own_ref, probs_ref, dlog_ref
):
    block_id = block_ref[0]
    first = pl.multiple_of((block_id % CORES) * TOK, TOK)
    kv = kv_ref[pl.ds(first, SPAN), :]
    keys, values = kv[:, :HD], kv[:, HD:]
    keys_t = keys.astype(jnp.float32).T.astype(jnp.bfloat16)
    for pair in range(GROUP // PAIR):
        queries = stacked(normed_ref, pair * PAIR, PAIR)
        upper = stacked(upper_ref, pair * PAIR, PAIR)
        scores = masked_scores(keys, queries, block_id)
        grad_probs = lax.dot_general(
            values, upper, (((1,), (1,)), ((), ())), preferred_element_type=jnp.float32
        )
        top = jnp.max(scores, axis=0, keepdims=True)
        terms = jnp.exp2((scores - top) * (SCALE * LOG2E))
        inverse = 1.0 / jnp.sum(terms, axis=0, keepdims=True)
        row_dot = jnp.sum(terms * grad_probs, axis=0, keepdims=True) * inverse
        probs = terms * inverse
        at = pair * PAIR * TOK
        probs_ref[:, at : at + PAIR * TOK] = probs.astype(jnp.bfloat16)
        dlog_ref[:, at : at + PAIR * TOK] = (probs * ((grad_probs - row_dot) * SCALE)).astype(
            jnp.bfloat16
        )
    dlogits = dlog_ref[...]
    grad_keys = jnp.dot(dlogits, stacked(normed_ref, 0, GROUP), preferred_element_type=jnp.float32)
    grad_values = jnp.dot(
        probs_ref[...], stacked(upper_ref, 0, GROUP), preferred_element_type=jnp.float32
    )
    grad_query = jnp.dot(keys_t, dlogits, preferred_element_type=jnp.float32)
    for g in range(GROUP):
        dq_ref[:, g * HD : (g + 1) * HD] = grad_query[:, g * TOK : (g + 1) * TOK].T
    for slot, ref in enumerate((far_ref, near_ref, own_ref)):
        ref[:, :HD] = grad_keys[slot * TOK : (slot + 1) * TOK].astype(ref.dtype)
        ref[:, HD:] = grad_values[slot * TOK : (slot + 1) * TOK].astype(ref.dtype)


def backward_attention(block_id, normed, upper, kv):
    wide = GROUP * HD
    heads = pl.BlockSpec((TOK, wide), lambda h: (0, h))
    grads = pl.BlockSpec((TOK, 2 * HD), lambda h: (0, h))
    kv_width = kv.shape[1]
    return pl.pallas_call(
        backward_kernel,
        grid=(KVH,),
        in_specs=[
            pl.BlockSpec(memory_space=pltpu.SMEM),
            heads,
            heads,
            pl.BlockSpec((4 * TOK, 2 * HD), lambda h: (0, h)),
        ],
        out_specs=[heads, grads, grads, grads],
        out_shape=[
            jax.ShapeDtypeStruct(normed.shape, jnp.float32),
            jax.ShapeDtypeStruct((TOK, kv_width), jnp.bfloat16),
            jax.ShapeDtypeStruct((TOK, kv_width), jnp.bfloat16),
            jax.ShapeDtypeStruct((TOK, kv_width), jnp.float32),
        ],
        scratch_shapes=[
            pltpu.VMEM((SPAN, wide), jnp.bfloat16),
            pltpu.VMEM((SPAN, wide), jnp.bfloat16),
        ],
        compiler_params=pltpu.CompilerParams(vmem_limit_bytes=32 * 2**20),
        cost_estimate=pl.CostEstimate(
            flops=4 * 10**9, bytes_accessed=8 * 2**20, transcendentals=2 * 10**6
        ),
        name="backward_attention",
    )(block_id, normed, upper, kv)


def input_grad_kernel(
    block_ref, own_ref, near_ref, far_ref, w_mine_ref, w_other_ref, dq_ref, x_ref, upper_ref, gain_ref,
    up_ref, down_ref, gain_grad_ref, grad_kv_ref, inv_ref, inner_ref, grad_ref,
):
    step = pl.program_id(0)
    core = block_ref[0] % CORES
    half = w_mine_ref.shape[1]
    width = w_mine_ref.shape[0]
    features = x_ref.shape[1]

    @pl.when(step == 0)
    def _():
        grad_kv_ref[...] = (
            own_ref[...] + near_ref[...].astype(jnp.float32) + far_ref[...].astype(jnp.float32)
        ).astype(jnp.bfloat16)
        squares = jnp.zeros((TOK, 1), jnp.float32)
        for at in range(0, features, width):
            part = x_ref[:, at : at + width].astype(jnp.float32)
            squares += jnp.sum(part * part, axis=-1, keepdims=True)
        inv_ref[...] = jnp.broadcast_to(lax.rsqrt(squares / features + EPSILON), inv_ref.shape)
        inner_ref[...] = jnp.zeros_like(inner_ref)

    at = pl.ds(pl.multiple_of(step * width, width), width)
    mine = grad_kv_ref[:, pl.ds(pl.multiple_of(core * half, half), half)]
    other = grad_kv_ref[:, pl.ds(pl.multiple_of((1 - core) * half, half), half)]
    contract = (((1,), (1,)), ((), ()))
    grad = dq_ref[...]
    grad += lax.dot_general(mine, w_mine_ref[...], contract, preferred_element_type=jnp.float32)
    grad += lax.dot_general(other, w_other_ref[...], contract, preferred_element_type=jnp.float32)
    inv_rms = inv_ref[:, :1]
    scaled = x_ref[:, at].astype(jnp.float32) * inv_rms
    gain_grad_ref[:, at] = jnp.sum(grad * scaled, axis=0, keepdims=True)
    grad = grad * gain_ref[:, at]
    grad_ref[:, at] = grad
    inner_ref[...] += jnp.broadcast_to(
        jnp.sum(grad * scaled, axis=-1, keepdims=True), inner_ref.shape
    )

    @pl.when(step == pl.num_programs(0) - 1)
    def _():
        for first, ref in ((0, up_ref), (TOK // 2, down_ref)):
            rows = slice(first, first + TOK // 2)
            inv = inv_ref[rows, :1]
            mean = inner_ref[rows, :1] * (1.0 / features)
            for at in range(0, features, width):
                cols = slice(at, at + width)
                scaled = x_ref[rows, cols].astype(jnp.float32) * inv
                out = inv * (grad_ref[rows, cols] - scaled * mean)
                ref[:, cols] = (out + upper_ref[rows, cols].astype(jnp.float32)).astype(jnp.bfloat16)


def input_grad(block_id, own, near, far, w_mine, w_other, dq, x, upper, gain_row):
    features, half = w_mine.shape
    width = 512
    whole = lambda shape: pl.BlockSpec(shape, lambda j: (0, 0))
    tokens = whole((TOK, features))
    return pl.pallas_call(
        input_grad_kernel,
        grid=(features // width,),
        in_specs=[
            pl.BlockSpec(memory_space=pltpu.SMEM),
            whole(own.shape),
            whole(own.shape),
            whole(own.shape),
            pl.BlockSpec((width, half), lambda j: (j, 0)),
            pl.BlockSpec((width, half), lambda j: (j, 0)),
            pl.BlockSpec((TOK, width), lambda j: (0, j)),
            tokens,
            tokens,
            whole((1, features)),
        ],
        out_specs=[
            whole((TOK // 2, features)),
            whole((TOK // 2, features)),
            whole((1, features)),
        ],
        out_shape=[
            jax.ShapeDtypeStruct((TOK // 2, features), jnp.bfloat16),
            jax.ShapeDtypeStruct((TOK // 2, features), jnp.bfloat16),
            jax.ShapeDtypeStruct((1, features), jnp.float32),
        ],
        scratch_shapes=[
            pltpu.VMEM((TOK, 2 * half), jnp.bfloat16),
            pltpu.VMEM((TOK, HD), jnp.float32),
            pltpu.VMEM((TOK, HD), jnp.float32),
            pltpu.VMEM((TOK, features), jnp.float32),
        ],
        compiler_params=pltpu.CompilerParams(vmem_limit_bytes=32 * 2**20),
        cost_estimate=pl.CostEstimate(
            flops=2 * 10**9, bytes_accessed=16 * 2**20, transcendentals=10**3
        ),
        name="input_grad",
    )(block_id, own, near, far, w_mine, w_other, dq, x, upper, gain_row)


def sum_over_ctx(value):
    moves = [lambda y, z, c: (y, z, c ^ 1)]
    moves += [lambda y, z, c, bit=bit: (y, z ^ bit, c) for bit in (1, 2)]
    moves += [lambda y, z, c, bit=bit: (y ^ bit, z, c) for bit in (1, 2, 4)]
    for move in moves:
        value = value + over_ctx(value, move)
    return value


def body(section_in, back_in, upstream, gains, kv_weight):
    index = lax.axis_index("ctx")
    core, z_lo, y = index % CORES, (index // CORES) % Z_LO, index // (CORES * Z_LO)
    block_id = index.astype(jnp.int32).reshape(1)
    x_back, upper_in = back_in[0], upstream[0]

    def start_crossing(after):
        x_fwd, _ = lax.optimization_barrier((section_in[0], after))
        return set_out(x_fwd[: TOK // 2], x_fwd[TOK // 2 :])

    w_mine, crossing = gather_weight(kv_weight[0], core, z_lo, y, start_crossing)
    x_parts = land(crossing, 1)
    peers = lax.axis_size("section")
    next_section = [(i, (i + 1) % peers) for i in range(peers)]
    gain_here = lax.ppermute(gains, "section", next_section)

    normed_back = norm_forward(x_back, gains)
    normed_fwd = norm_forward(section_in[0], gains)
    partner = swap(jnp.concatenate([normed_back, normed_fwd], axis=0))
    chip_back = chip_rows(normed_back, partner[:TOK], core)
    chip_fwd = chip_rows(normed_fwd, partner[TOK:], core)

    def project(normed):
        return jnp.dot(normed, w_mine, preferred_element_type=jnp.float32).astype(jnp.bfloat16)

    kv_back, x_parts = lax.optimization_barrier((project(chip_back), x_parts))
    x_here = jnp.concatenate(x_parts, axis=0)
    window_back = window(kv_back, core)
    kv_fwd, w_later, _ = lax.optimization_barrier((project(chip_fwd), w_mine, window_back))
    w_other = swap(w_later)
    kv_here = lax.ppermute(kv_fwd, "section", next_section)

    dq, far, near, own = backward_attention(block_id, normed_back, upper_in, window_back)
    kv_here, near, far = lax.optimization_barrier((kv_here, near, far))
    near = lax.ppermute(near, "ctx", [(i, i - 1) for i in range(1, CTX)])
    far = lax.ppermute(far, "ctx", [(i, i - 2) for i in range(2, CTX)])
    up, down, gain_part = input_grad(
        block_id, own, near, far, w_mine, w_other, dq, x_back, upper_in, gains
    )
    next_grad = jnp.concatenate(land(set_out(up, down), -1), axis=0)
    gain_total = sum_over_ctx(gain_part)

    window_here = window(kv_here, core)
    x_here, _ = lax.optimization_barrier((x_here, up))
    next_in = forward_attention(block_id, norm_forward(x_here, gain_here), x_here, window_here)
    return (next_in[None], next_grad[None], gain_total)


def solution(mesh):
    in_specs = (
        P("section", "ctx", None),
        P("section", "ctx", None),
        P("section", "ctx", None),
        P("section", None),
        P("section", "ctx", None),
    )
    out_specs = (P("section", "ctx", None), P("section", "ctx", None), P("section", None))
    return jax.shard_map(body, mesh=mesh, in_specs=in_specs, out_specs=out_specs, check_vma=False)
```

```python
import functools

import jax
import jax.numpy as jnp
from jax import lax
from jax.experimental import pallas as pl
from jax.experimental.pallas import tpu as pltpu
from jax.sharding import PartitionSpec as P

HD = 128
STEPS = 2
EPSILON = 1e-05
GROUP = 8
KVH = 4
TOK = 128
SPAN = (STEPS + 1) * TOK

X, Z_HI, Y, Z_LO, CORES = 4, 2, 8, 4, 2
Z = Z_HI * Z_LO
CHIPS = Y * Z_LO
CTX = Y * Z_LO * CORES

HEADS = KVH // CORES
CHIP_TOK = CORES * TOK
HALF = HEADS * GROUP * HD

SCALE = HD ** (-0.5)
LOG2E = 1.4426950408889634


def ctx_pairs(move):
    pairs = []
    for c in range(CTX):
        target = move(c // (Z_LO * CORES), (c // CORES) % Z_LO, c % CORES)
        if target is not None:
            y, z_lo, core = target
            pairs.append((c, (y * Z_LO + z_lo) * CORES + core))
    return pairs


def over_ctx(value, move):
    return lax.ppermute(value, "ctx", ctx_pairs(move))


def grid_pairs(move):
    pairs = []
    for x in range(X):
        for z in range(Z):
            new_x, new_z = move(x, z)
            new_x, new_z = (new_x % X, new_z % Z)
            for y in range(Y):
                for core in range(CORES):
                    source = (x * Z_HI + z // Z_LO) * CTX + (y * Z_LO + z % Z_LO) * CORES + core
                    target = (new_x * Z_HI + new_z // Z_LO) * CTX + (y * Z_LO + new_z % Z_LO) * CORES + core
                    pairs.append((source, target))
    return pairs


def over_grid(value, move):
    return lax.ppermute(value, ("section", "ctx"), grid_pairs(move))


def halfway(value, way):
    return over_grid(value, lambda x, z: (x, z + 2 * way))


def arrive(value, way, distance):
    def move(x, z):
        z_hi = ((z - 2 * way) % Z) // Z_LO
        cross = (1 if z_hi == Z_HI - 1 else 0) if distance == 1 else (-1 if z_hi == 0 else 0)
        return (x + cross, z + 2 * way)

    return over_grid(value, move)


def set_out(upper, lower):
    return halfway(upper, 1), halfway(lower, -1)


def land(halves, distance):
    return arrive(halves[0], 1, distance), arrive(halves[1], -1, distance)


def norm_forward(section_x, gain_row):
    values = section_x.astype(jnp.float32)
    inv_rms = lax.rsqrt(jnp.mean(values * values, axis=-1, keepdims=True) + EPSILON)
    return (values * inv_rms * gain_row).astype(jnp.bfloat16)


def by_head(kv_columns):
    parts = []
    for head in range(KVH):
        parts.append(kv_columns[:, head * HD : (head + 1) * HD])
        parts.append(kv_columns[:, (KVH + head) * HD : (KVH + head + 1) * HD])
    return jnp.concatenate(parts, axis=1)


def gather_weight(own_rows, core):
    half = own_rows.shape[1] // 2
    columns = by_head(own_rows)
    low, high = columns[:, :half], columns[:, half:]
    keep = jnp.where(core == 0, low, high)
    received = swap(jnp.where(core == 0, high, low))
    chip = chip_rows(keep, received, core)
    same_core = [[chip * CORES + c for chip in range(Y * Z_LO)] for c in range(CORES)]
    return lax.all_gather(chip, "ctx", axis_index_groups=same_core, axis=0, tiled=True)


def swap(value):
    return over_ctx(value, lambda y, z, c: (y, z, 1 - c))


def chip_rows(own, partner, core):
    return jnp.concatenate(
        [jnp.where(core == 0, own, partner), jnp.where(core == 0, partner, own)], axis=0
    )


def to_next_chip(value):
    pairs = [(i, i + CORES) for i in range(CTX - CORES)]
    return lax.ppermute(value, "ctx", pairs)


def to_chip_before(value):
    pairs = [(i, i - CORES) for i in range(CORES, CTX)]
    return lax.ppermute(value, "ctx", pairs)


def columns_of(value, core):
    return lax.dynamic_slice_in_dim(value, core * HALF, HALF, 1)


def chip_columns(value, core):
    return chip_rows(columns_of(value, core), swap(columns_of(value, 1 - core)), core)


def stacked(ref, tokens):
    rows = slice(tokens * TOK, (tokens + 1) * TOK)
    return jnp.concatenate([ref[rows, g * HD : (g + 1) * HD] for g in range(GROUP)], axis=0)


def masked_scores(keys, queries, tokens, any_before):
    scores = lax.dot_general(
        keys, queries, (((1,), (1,)), ((), ())), preferred_element_type=jnp.float32
    )
    across = queries.shape[0]
    before = (STEPS - tokens) * TOK
    seen = lax.broadcasted_iota(jnp.int32, (TOK, across), 0)
    query = lax.broadcasted_iota(jnp.int32, (TOK, across), 1) % TOK
    parts = [jnp.where(any_before, scores[:before], -1e30)]
    if tokens:
        parts.append(scores[before : STEPS * TOK])
    parts.append(jnp.where(seen <= query, scores[STEPS * TOK :], -1e30))
    return jnp.concatenate(parts, axis=0)


PAIR = 2
WIDE = GROUP * HD


def forward_kernel(index_ref, normed_ref, x_ref, before_ref, own_ref, out_ref):
    any_before = index_ref[0] >= CORES
    keys = jnp.concatenate([before_ref[:, :HD], own_ref[:, :HD]], axis=0)
    values = jnp.concatenate([before_ref[:, HD:], own_ref[:, HD:]], axis=0)
    values_t = values.astype(jnp.float32).T.astype(jnp.bfloat16)
    for tokens in range(CORES):
        span = slice(tokens * TOK, tokens * TOK + SPAN)
        rows = slice(tokens * TOK, (tokens + 1) * TOK)
        queries = stacked(normed_ref, tokens)
        for pair in range(GROUP // PAIR):
            these = queries[pair * PAIR * TOK : (pair + 1) * PAIR * TOK]
            scores = masked_scores(keys[span], these, tokens, any_before)
            top = jnp.max(scores, axis=0, keepdims=True)
            terms = jnp.exp2((scores - top) * (SCALE * LOG2E))
            total = jnp.sum(terms, axis=0, keepdims=True)
            attended = jnp.dot(
                values_t[:, span], terms.astype(jnp.bfloat16), preferred_element_type=jnp.float32
            ) * (1.0 / total)
            for g in range(PAIR):
                at = (pair * PAIR + g) * HD
                cols = slice(at, at + HD)
                out = attended[:, g * TOK : (g + 1) * TOK].T + x_ref[rows, cols].astype(jnp.float32)
                out_ref[rows, cols] = out.astype(jnp.bfloat16)


def forward_attention(index, normed, x, before, own):
    heads = pl.BlockSpec((CHIP_TOK, WIDE), lambda h, index: (0, h))
    kv = pl.BlockSpec((CHIP_TOK, 2 * HD), lambda h, index: (0, h))
    return pl.pallas_call(
        forward_kernel,
        grid_spec=pltpu.PrefetchScalarGridSpec(
            num_scalar_prefetch=1,
            grid=(HEADS,),
            in_specs=[heads, heads, kv, kv],
            out_specs=heads,
        ),
        out_shape=jax.ShapeDtypeStruct(x.shape, jnp.bfloat16),
        compiler_params=pltpu.CompilerParams(vmem_limit_bytes=32 * 2**20),
        cost_estimate=pl.CostEstimate(
            flops=4 * 10**9, bytes_accessed=8 * 2**20, transcendentals=2 * 10**6
        ),
        name="forward_attention",
    )(index, normed, x, before, own)


def backward_kernel(
    index_ref, normed_ref, upper_ref, before_ref, own_ref, dq_ref, grad_before_ref, grad_own_ref,
    probs_ref, dlog_ref,
):
    any_before = index_ref[0] >= CORES
    keys = jnp.concatenate([before_ref[:, :HD], own_ref[:, :HD]], axis=0)
    values = jnp.concatenate([before_ref[:, HD:], own_ref[:, HD:]], axis=0)
    keys_t = keys.astype(jnp.float32).T.astype(jnp.bfloat16)
    queries = [stacked(normed_ref, tokens) for tokens in range(CORES)]
    uppers = [stacked(upper_ref, tokens) for tokens in range(CORES)]
    for tokens in range(CORES):
        span = slice(tokens * TOK, tokens * TOK + SPAN)
        for pair in range(GROUP // PAIR):
            these = slice(pair * PAIR * TOK, (pair + 1) * PAIR * TOK)
            scores = masked_scores(keys[span], queries[tokens][these], tokens, any_before)
            grad_probs = lax.dot_general(
                values[span],
                uppers[tokens][these],
                (((1,), (1,)), ((), ())),
                preferred_element_type=jnp.float32,
            )
            top = jnp.max(scores, axis=0, keepdims=True)
            terms = jnp.exp2((scores - top) * (SCALE * LOG2E))
            inverse = 1.0 / jnp.sum(terms, axis=0, keepdims=True)
            row_dot = jnp.sum(terms * grad_probs, axis=0, keepdims=True) * inverse
            probs = terms * inverse
            cols = slice(tokens * WIDE + these.start, tokens * WIDE + these.stop)
            probs_ref[span, cols] = probs.astype(jnp.bfloat16)
            dlog_ref[span, cols] = (probs * ((grad_probs - row_dot) * SCALE)).astype(jnp.bfloat16)
        dlogits = dlog_ref[span, tokens * WIDE : (tokens + 1) * WIDE]
        grad_query = jnp.dot(keys_t[:, span], dlogits, preferred_element_type=jnp.float32)
        rows = slice(tokens * TOK, (tokens + 1) * TOK)
        for g in range(GROUP):
            dq_ref[rows, g * HD : (g + 1) * HD] = grad_query[:, g * TOK : (g + 1) * TOK].T
    for left, factors, first in ((dlog_ref, queries, 0), (probs_ref, uppers, HD)):
        cols = slice(first, first + HD)

        def product(rows, tokens, last):
            factor = jnp.concatenate(factors[tokens:last], axis=0)
            return jnp.dot(
                left[rows, tokens * WIDE : last * WIDE], factor, preferred_element_type=jnp.float32
            )

        middle = product(slice(TOK, 3 * TOK), 0, 2)
        grad_before_ref[:TOK, cols] = product(slice(0, TOK), 0, 1).astype(jnp.bfloat16)
        grad_before_ref[TOK:, cols] = middle[:TOK].astype(jnp.bfloat16)
        grad_own_ref[:TOK, cols] = middle[TOK:]
        grad_own_ref[TOK:, cols] = product(slice(3 * TOK, 4 * TOK), 1, 2)


def backward_attention(index, normed, upper, before, own):
    kv = pl.BlockSpec((CHIP_TOK, 2 * HD), lambda h, index: (0, h))
    heads = pl.BlockSpec((CHIP_TOK, WIDE), lambda h, index: (0, h))
    return pl.pallas_call(
        backward_kernel,
        grid_spec=pltpu.PrefetchScalarGridSpec(
            num_scalar_prefetch=1,
            grid=(HEADS,),
            in_specs=[
                pl.BlockSpec((CHIP_TOK, WIDE), lambda h, index: (0, (index[0] % CORES) * HEADS + h)),
                heads,
                kv,
                kv,
            ],
            out_specs=[heads, kv, kv],
            scratch_shapes=[
                pltpu.VMEM((4 * TOK, CORES * WIDE), jnp.bfloat16),
                pltpu.VMEM((4 * TOK, CORES * WIDE), jnp.bfloat16),
            ],
        ),
        out_shape=[
            jax.ShapeDtypeStruct((CHIP_TOK, HALF), jnp.float32),
            jax.ShapeDtypeStruct(before.shape, jnp.bfloat16),
            jax.ShapeDtypeStruct(own.shape, jnp.float32),
        ],
        compiler_params=pltpu.CompilerParams(vmem_limit_bytes=40 * 2**20),
        cost_estimate=pl.CostEstimate(
            flops=4 * 10**9, bytes_accessed=8 * 2**20, transcendentals=2 * 10**6
        ),
        name="backward_attention",
    )(index, normed, upper, before, own)


def partial_kernel(where_ref, own_ref, after_ref, weight_ref, dq_ref, out_ref, grad_kv_ref):
    step = pl.program_id(0)
    steps = pl.num_programs(0) // CORES

    @pl.when(step == 0)
    def _():
        grad_kv_ref[...] = (own_ref[...] + after_ref[...].astype(jnp.float32)).astype(jnp.bfloat16)

    product = lax.dot_general(
        grad_kv_ref[...], weight_ref[...], (((1,), (1,)), ((), ())), preferred_element_type=jnp.float32
    )
    here = step // steps == where_ref[1]

    @pl.when(here)
    def _():
        out_ref[...] = (product + dq_ref[...]).astype(out_ref.dtype)

    @pl.when(jnp.logical_not(here))
    def _():
        out_ref[...] = product.astype(out_ref.dtype)


def partial_grad(row, core, own, after, weight, dq, kind):
    features, half = weight.shape
    width = 1024
    steps = features // width // CORES
    rows = pl.BlockSpec((TOK, half), lambda j, where: (where[0], 0))
    return pl.pallas_call(
        partial_kernel,
        grid_spec=pltpu.PrefetchScalarGridSpec(
            num_scalar_prefetch=1,
            grid=(features // width,),
            in_specs=[
                rows,
                rows,
                pl.BlockSpec((width, half), lambda j, where: (j, 0)),
                pl.BlockSpec((TOK, width), lambda j, where: (where[0], j % steps)),
            ],
            out_specs=pl.BlockSpec((TOK, width), lambda j, where: (0, j)),
            scratch_shapes=[pltpu.VMEM((TOK, half), jnp.bfloat16)],
        ),
        out_shape=jax.ShapeDtypeStruct((TOK, features), kind),
        compiler_params=pltpu.CompilerParams(vmem_limit_bytes=32 * 2**20),
        cost_estimate=pl.CostEstimate(
            flops=10**9, bytes_accessed=8 * 2**20, transcendentals=0
        ),
        name="partial_grad",
    )(jnp.stack([row, core]).astype(jnp.int32), own, after, weight, dq)


def input_grad_kernel(
    own_ref, other_ref, x_ref, upper_ref, gain_ref, up_ref, down_ref, gain_grad_ref, grad_ref
):
    features = x_ref.shape[1]
    width = 512
    blocks = [slice(at, at + width) for at in range(0, features, width)]
    squares = jnp.zeros((TOK, 1), jnp.float32)
    for cols in blocks:
        part = x_ref[:, cols].astype(jnp.float32)
        squares += jnp.sum(part * part, axis=-1, keepdims=True)
    inv_rms = lax.rsqrt(squares / features + EPSILON)
    inner = jnp.zeros((TOK, 1), jnp.float32)
    for cols in blocks:
        grad = own_ref[:, cols] + other_ref[:, cols].astype(jnp.float32)
        scaled = x_ref[:, cols].astype(jnp.float32) * inv_rms
        product = grad * scaled
        gain_grad_ref[:, cols] = jnp.sum(product, axis=0, keepdims=True)
        gain = gain_ref[:, cols]
        inner += jnp.sum(product * gain, axis=-1, keepdims=True)
        grad_ref[:, cols] = grad * gain
    mean = inner * (1.0 / features)
    for first, ref in ((0, up_ref), (TOK // 2, down_ref)):
        rows = slice(first, first + TOK // 2)
        inv = inv_rms[rows]
        for cols in blocks:
            scaled = x_ref[rows, cols].astype(jnp.float32) * inv
            out = inv * (grad_ref[rows, cols] - scaled * mean[rows])
            ref[:, cols] = (out + upper_ref[rows, cols].astype(jnp.float32)).astype(jnp.bfloat16)


def input_grad(own, other, x, upper, gain_row):
    features = x.shape[1]
    return pl.pallas_call(
        input_grad_kernel,
        out_shape=[
            jax.ShapeDtypeStruct((TOK // 2, features), jnp.bfloat16),
            jax.ShapeDtypeStruct((TOK // 2, features), jnp.bfloat16),
            jax.ShapeDtypeStruct((1, features), jnp.float32),
        ],
        scratch_shapes=[pltpu.VMEM((TOK, features), jnp.float32)],
        compiler_params=pltpu.CompilerParams(vmem_limit_bytes=32 * 2**20),
        cost_estimate=pl.CostEstimate(
            flops=10**7, bytes_accessed=8 * 2**20, transcendentals=10**3
        ),
        name="input_grad",
    )(own, other, x, upper, gain_row)


def body(section_in, back_in, upstream, gains, kv_weight):
    index = lax.axis_index("ctx").astype(jnp.int32)
    core = index % CORES
    place = index.reshape(1)
    x_back, upper_in = back_in[0], upstream[0]

    w_mine = gather_weight(kv_weight[0], core)
    x_parts = land(set_out(section_in[0, : TOK // 2], section_in[0, TOK // 2 :]), 1)
    peers = lax.axis_size("section")
    next_section = [(i, (i + 1) % peers) for i in range(peers)]
    gain_here = lax.ppermute(gains, "section", next_section)

    normed_back = norm_forward(x_back, gains)
    normed_fwd = norm_forward(section_in[0], gains)
    partner = swap(jnp.concatenate([normed_back, normed_fwd], axis=0))
    chip_back = chip_rows(normed_back, partner[:TOK], core)
    chip_fwd = chip_rows(normed_fwd, partner[TOK:], core)
    chip_upper = chip_columns(upper_in, core)

    x_here = jnp.concatenate(x_parts, axis=0)
    normed_here = norm_forward(x_here, gain_here)
    swapped = swap(
        jnp.concatenate([columns_of(normed_here, 1 - core), columns_of(x_here, 1 - core)], axis=0)
    )
    chip_normed_here = chip_rows(columns_of(normed_here, core), swapped[:TOK], core)
    chip_x_here = chip_rows(columns_of(x_here, core), swapped[TOK:], core)

    chip_back, chip_fwd, chip_upper, chip_normed_here, chip_x_here = lax.optimization_barrier(
        (chip_back, chip_fwd, chip_upper, chip_normed_here, chip_x_here)
    )

    def project(normed):
        return jnp.dot(normed, w_mine, preferred_element_type=jnp.float32).astype(jnp.bfloat16)

    kv_back = project(chip_back)
    before = to_next_chip(kv_back)
    kv_fwd = project(chip_fwd)
    kv_here = lax.ppermute(kv_fwd, "section", next_section)

    dq, grad_before, grad_own = backward_attention(place, chip_back, chip_upper, before, kv_back)
    after, kv_here = lax.optimization_barrier((to_chip_before(grad_before), kv_here))
    before_here = to_next_chip(kv_here)

    away = partial_grad(1 - core, core, grad_own, after, w_mine, dq, jnp.bfloat16)
    home = partial_grad(core, core, grad_own, after, w_mine, dq, jnp.float32)
    away, home, before_here = lax.optimization_barrier((swap(away), home, before_here))
    up, down, gain_part = input_grad(home, away, x_back, upper_in, gains)
    next_grad = jnp.concatenate(land(set_out(up, down), -1), axis=0)
    gain_total = jnp.sum(
        lax.all_gather(gain_part, "ctx", axis=0, tiled=True), axis=0, keepdims=True
    )

    chip_x_here, _ = lax.optimization_barrier((chip_x_here, up))
    out = forward_attention(place, chip_normed_here, chip_x_here, before_here, kv_here)
    first, second = out[:TOK], out[TOK:]
    mine = jnp.where(core == 0, first, second)
    other = swap(jnp.where(core == 0, second, first))
    next_in = jnp.concatenate(
        [jnp.where(core == 0, mine, other), jnp.where(core == 0, other, mine)], axis=1
    )
    return (next_in[None], next_grad[None], gain_total)


def solution(mesh):
    in_specs = (
        P("section", "ctx", None),
        P("section", "ctx", None),
        P("section", "ctx", None),
        P("section", None),
        P("section", "ctx", None),
    )
    out_specs = (P("section", "ctx", None), P("section", "ctx", None), P("section", None))
    return jax.shard_map(body, mesh=mesh, in_specs=in_specs, out_specs=out_specs, check_vma=False)
```

```python
import functools

import jax
import jax.numpy as jnp
from jax import lax
from jax.experimental import pallas as pl
from jax.experimental.pallas import tpu as pltpu
from jax.sharding import PartitionSpec as P

HD = 128
STEPS = 2
EPSILON = 1e-05
GROUP = 8
KVH = 4
TOK = 128
SPAN = (STEPS + 1) * TOK

X, Z_HI, Y, Z_LO, CORES = 4, 2, 8, 4, 2
Z = Z_HI * Z_LO
CHIPS = Y * Z_LO
CTX = Y * Z_LO * CORES

HEADS = KVH // CORES
CHIP_TOK = CORES * TOK
HALF = HEADS * GROUP * HD

SCALE = HD ** (-0.5)
LOG2E = 1.4426950408889634


def ctx_pairs(move):
    pairs = []
    for c in range(CTX):
        target = move(c // (Z_LO * CORES), (c // CORES) % Z_LO, c % CORES)
        if target is not None:
            y, z_lo, core = target
            pairs.append((c, (y * Z_LO + z_lo) * CORES + core))
    return pairs


def over_ctx(value, move):
    return lax.ppermute(value, "ctx", ctx_pairs(move))


def grid_pairs(move):
    pairs = []
    for x in range(X):
        for z in range(Z):
            new_x, new_z = move(x, z)
            new_x, new_z = (new_x % X, new_z % Z)
            for y in range(Y):
                for core in range(CORES):
                    source = (x * Z_HI + z // Z_LO) * CTX + (y * Z_LO + z % Z_LO) * CORES + core
                    target = (new_x * Z_HI + new_z // Z_LO) * CTX + (y * Z_LO + new_z % Z_LO) * CORES + core
                    pairs.append((source, target))
    return pairs


def over_grid(value, move):
    return lax.ppermute(value, ("section", "ctx"), grid_pairs(move))


def halfway(value, way):
    return over_grid(value, lambda x, z: (x, z + 2 * way))


def arrive(value, way, distance):
    def move(x, z):
        z_hi = ((z - 2 * way) % Z) // Z_LO
        cross = (1 if z_hi == Z_HI - 1 else 0) if distance == 1 else (-1 if z_hi == 0 else 0)
        return (x + cross, z + 2 * way)

    return over_grid(value, move)


def direct(value, distance):
    peers = Z_HI * X
    return lax.ppermute(value, "section", [(i, (i + distance) % peers) for i in range(peers)])


def norm_forward(section_x, gain_row):
    values = section_x.astype(jnp.float32)
    inv_rms = lax.rsqrt(jnp.mean(values * values, axis=-1, keepdims=True) + EPSILON)
    return (values * inv_rms * gain_row).astype(jnp.bfloat16), inv_rms


def by_head(kv_columns):
    parts = []
    for head in range(KVH):
        parts.append(kv_columns[:, head * HD : (head + 1) * HD])
        parts.append(kv_columns[:, (KVH + head) * HD : (KVH + head + 1) * HD])
    return jnp.concatenate(parts, axis=1)


def gather_run(own_rows, core, z_lo):
    half = own_rows.shape[1] // 2
    columns = by_head(own_rows)
    low, high = columns[:, :half], columns[:, half:]
    keep = jnp.where(core == 0, low, high)
    received = swap(jnp.where(core == 0, high, low))
    chip = chip_rows(keep, received, core)
    rows = chip.shape[0]
    pieces = [chip]
    for step in range(1, Z_LO):
        pieces.append(over_ctx(chip, lambda y, z, c, step=step: (y, (z + step) % Z_LO, c)))
    back = pieces[::-1]
    return lax.dynamic_slice_in_dim(
        jnp.concatenate(back + back[:-1], axis=0), (Z_LO - 1 - z_lo) * rows, Z_LO * rows, 0
    )


def gather_weight(run, set_out):
    def up(piece):
        return over_ctx(piece, lambda y, z, c: ((y + 1) % Y, z, c))

    def down(piece):
        return over_ctx(piece, lambda y, z, c: ((y - 1) % Y, z, c))

    first_out, second_out, first_in = set_out
    rising, falling = [up(run)], [down(run)]
    first = first_out(run)
    rising.append(up(rising[0]))
    falling.append(down(falling[0]))
    second = second_out(rising[0])
    rising[1], falling[1], first = lax.optimization_barrier((rising[1], falling[1], first))
    rising.append(up(rising[1]))
    falling.append(down(falling[1]))
    first = first_in(first)
    rising[2], falling[2], second = lax.optimization_barrier((rising[2], falling[2], second))
    middle = run.shape[0] // 2
    rising.append(up(rising[2][:middle]))
    falling.append(down(falling[2][middle:]))
    rising[3], falling[3], first = lax.optimization_barrier((rising[3], falling[3], first))
    pieces = [run, *falling[:3], rising[3], falling[3], *rising[:3][::-1]]
    return pieces, first, second


def swap(value):
    return over_ctx(value, lambda y, z, c: (y, z, 1 - c))


def chip_rows(own, partner, core):
    return jnp.concatenate(
        [jnp.where(core == 0, own, partner), jnp.where(core == 0, partner, own)], axis=0
    )


def to_next_chip(value):
    pairs = [(i, i + CORES) for i in range(CTX - CORES)]
    return lax.ppermute(value, "ctx", pairs)


def to_chip_before(value):
    pairs = [(i, i - CORES) for i in range(CORES, CTX)]
    return lax.ppermute(value, "ctx", pairs)


def columns_of(value, core):
    return lax.dynamic_slice_in_dim(value, core * HALF, HALF, 1)


def chip_columns(value, core):
    return chip_rows(columns_of(value, core), swap(columns_of(value, 1 - core)), core)


def stacked(ref, tokens):
    rows = slice(tokens * TOK, (tokens + 1) * TOK)
    return jnp.concatenate([ref[rows, g * HD : (g + 1) * HD] for g in range(GROUP)], axis=0)


def masked_scores(keys, queries, tokens, any_before):
    scores = lax.dot_general(
        keys, queries, (((1,), (1,)), ((), ())), preferred_element_type=jnp.float32
    )
    across = queries.shape[0]
    before = (STEPS - tokens) * TOK
    seen = lax.broadcasted_iota(jnp.int32, (TOK, across), 0)
    query = lax.broadcasted_iota(jnp.int32, (TOK, across), 1) % TOK
    parts = [jnp.where(any_before, scores[:before], -1e30)]
    if tokens:
        parts.append(scores[before : STEPS * TOK])
    parts.append(jnp.where(seen <= query, scores[STEPS * TOK :], -1e30))
    return jnp.concatenate(parts, axis=0)


PAIR = 2
WIDE = GROUP * HD

BRIEF = pl.CostEstimate(flops=1000, bytes_accessed=1000, transcendentals=0)


def forward_kernel(
    index_ref, first_ref, second_ref, inv_ref, gain_ref, before_ref, own_ref, out_ref
):
    any_before = index_ref[0] >= CORES
    keys = jnp.concatenate([before_ref[:, :HD], own_ref[:, :HD]], axis=0)
    values = jnp.concatenate([before_ref[:, HD:], own_ref[:, HD:]], axis=0)
    values_t = values.astype(jnp.float32).T.astype(jnp.bfloat16)
    for tokens, x_ref in enumerate((first_ref, second_ref)):
        span = slice(tokens * TOK, tokens * TOK + SPAN)
        rows = slice(tokens * TOK, (tokens + 1) * TOK)
        inv = inv_ref[rows, :]
        for pair in range(GROUP // PAIR):
            cols = [
                slice(g * HD, (g + 1) * HD) for g in range(pair * PAIR, (pair + 1) * PAIR)
            ]
            x = [x_ref[:, at].astype(jnp.float32) for at in cols]
            queries = jnp.concatenate(
                [(part * inv * gain_ref[:, at]).astype(jnp.bfloat16) for part, at in zip(x, cols)],
                axis=0,
            )
            scores = masked_scores(keys[span], queries, tokens, any_before)
            top = jnp.max(scores, axis=0, keepdims=True)
            terms = jnp.exp2((scores - top) * (SCALE * LOG2E))
            total = jnp.sum(terms, axis=0, keepdims=True)
            attended = jnp.dot(
                values_t[:, span], terms.astype(jnp.bfloat16), preferred_element_type=jnp.float32
            ) * (1.0 / total)
            for g, at in enumerate(cols):
                out = attended[:, g * TOK : (g + 1) * TOK].T + x[g]
                out_ref[rows, at] = out.astype(jnp.bfloat16)


def forward_attention(index, first, second, inv_rms, gain, before, own):
    heads = pl.BlockSpec((CHIP_TOK, WIDE), lambda h, index: (0, h))
    tokens = pl.BlockSpec((TOK, WIDE), lambda h, index: (0, h))
    kv = pl.BlockSpec((CHIP_TOK, 2 * HD), lambda h, index: (0, h))
    return pl.pallas_call(
        forward_kernel,
        grid_spec=pltpu.PrefetchScalarGridSpec(
            num_scalar_prefetch=1,
            grid=(HEADS,),
            in_specs=[
                tokens,
                tokens,
                pl.BlockSpec((CHIP_TOK, 1), lambda h, index: (0, 0)),
                pl.BlockSpec((1, WIDE), lambda h, index: (0, h)),
                kv,
                kv,
            ],
            out_specs=heads,
        ),
        out_shape=jax.ShapeDtypeStruct((CHIP_TOK, HALF), jnp.bfloat16),
        compiler_params=pltpu.CompilerParams(vmem_limit_bytes=32 * 2**20),
        cost_estimate=BRIEF,
        name="forward_attention",
    )(index, first, second, inv_rms, gain, before, own)


def backward_kernel(
    index_ref, normed_ref, upper_ref, before_ref, own_ref, dq_ref, grad_before_ref, grad_own_ref,
    probs_ref, dlog_ref,
):
    any_before = index_ref[0] >= CORES
    keys = jnp.concatenate([before_ref[:, :HD], own_ref[:, :HD]], axis=0)
    values = jnp.concatenate([before_ref[:, HD:], own_ref[:, HD:]], axis=0)
    keys_t = keys.astype(jnp.float32).T.astype(jnp.bfloat16)
    queries = [stacked(normed_ref, tokens) for tokens in range(CORES)]
    uppers = [stacked(upper_ref, tokens) for tokens in range(CORES)]
    for tokens in range(CORES):
        span = slice(tokens * TOK, tokens * TOK + SPAN)
        for pair in range(GROUP // PAIR):
            these = slice(pair * PAIR * TOK, (pair + 1) * PAIR * TOK)
            scores = masked_scores(keys[span], queries[tokens][these], tokens, any_before)
            grad_probs = lax.dot_general(
                values[span],
                uppers[tokens][these],
                (((1,), (1,)), ((), ())),
                preferred_element_type=jnp.float32,
            )
            top = jnp.max(scores, axis=0, keepdims=True)
            terms = jnp.exp2((scores - top) * (SCALE * LOG2E))
            inverse = 1.0 / jnp.sum(terms, axis=0, keepdims=True)
            row_dot = jnp.sum(terms * grad_probs, axis=0, keepdims=True) * inverse
            probs = terms * inverse
            cols = slice(tokens * WIDE + these.start, tokens * WIDE + these.stop)
            probs_ref[span, cols] = probs.astype(jnp.bfloat16)
            dlog_ref[span, cols] = (probs * ((grad_probs - row_dot) * SCALE)).astype(jnp.bfloat16)
        dlogits = dlog_ref[span, tokens * WIDE : (tokens + 1) * WIDE]
        grad_query = jnp.dot(keys_t[:, span], dlogits, preferred_element_type=jnp.float32)
        rows = slice(tokens * TOK, (tokens + 1) * TOK)
        for g in range(GROUP):
            dq_ref[rows, g * HD : (g + 1) * HD] = grad_query[:, g * TOK : (g + 1) * TOK].T
    for left, factors, first in ((dlog_ref, queries, 0), (probs_ref, uppers, HD)):
        cols = slice(first, first + HD)

        def product(rows, tokens, last):
            factor = jnp.concatenate(factors[tokens:last], axis=0)
            return jnp.dot(
                left[rows, tokens * WIDE : last * WIDE], factor, preferred_element_type=jnp.float32
            )

        middle = product(slice(TOK, 3 * TOK), 0, 2)
        grad_before_ref[:TOK, cols] = product(slice(0, TOK), 0, 1).astype(jnp.bfloat16)
        grad_before_ref[TOK:, cols] = middle[:TOK].astype(jnp.bfloat16)
        grad_own_ref[:TOK, cols] = middle[TOK:]
        grad_own_ref[TOK:, cols] = product(slice(3 * TOK, 4 * TOK), 1, 2)


def backward_attention(index, normed, upper, before, own):
    kv = pl.BlockSpec((CHIP_TOK, 2 * HD), lambda h, index: (0, h))
    heads = pl.BlockSpec((CHIP_TOK, WIDE), lambda h, index: (0, h))
    return pl.pallas_call(
        backward_kernel,
        grid_spec=pltpu.PrefetchScalarGridSpec(
            num_scalar_prefetch=1,
            grid=(HEADS,),
            in_specs=[
                pl.BlockSpec((CHIP_TOK, WIDE), lambda h, index: (0, (index[0] % CORES) * HEADS + h)),
                heads,
                kv,
                kv,
            ],
            out_specs=[heads, kv, kv],
            scratch_shapes=[
                pltpu.VMEM((4 * TOK, CORES * WIDE), jnp.bfloat16),
                pltpu.VMEM((4 * TOK, CORES * WIDE), jnp.bfloat16),
            ],
        ),
        out_shape=[
            jax.ShapeDtypeStruct((CHIP_TOK, HALF), jnp.float32),
            jax.ShapeDtypeStruct(before.shape, jnp.bfloat16),
            jax.ShapeDtypeStruct(own.shape, jnp.float32),
        ],
        compiler_params=pltpu.CompilerParams(vmem_limit_bytes=40 * 2**20),
        cost_estimate=BRIEF,
        name="backward_attention",
    )(index, normed, upper, before, own)


def piece_columns(y, pieces):
    firsts, at = [], 0
    block = pieces[0].shape[0]
    for piece in pieces:
        firsts.append(pl.multiple_of(((y + at // block) % Y) * block, block) + at % block)
        at += piece.shape[0]
    return firsts


def project_kernel(y_ref, normed_ref, *refs):
    *pieces, out_ref = refs
    total = jnp.zeros(out_ref.shape, jnp.float32)
    for first, piece in zip(piece_columns(y_ref[0], pieces), pieces):
        rows = piece.shape[0]
        part = normed_ref[:, pl.ds(pl.multiple_of(first, rows), rows)]
        total += jnp.dot(part, piece[...], preferred_element_type=jnp.float32)
    out_ref[...] = total.astype(out_ref.dtype)


SCALARS = pl.BlockSpec(memory_space=pltpu.SMEM)
WHOLE = pl.BlockSpec(memory_space=pltpu.VMEM)


def project(y, normed, pieces):
    return pl.pallas_call(
        project_kernel,
        in_specs=[SCALARS] + [WHOLE] * (1 + len(pieces)),
        out_specs=WHOLE,
        out_shape=jax.ShapeDtypeStruct((normed.shape[0], pieces[0].shape[1]), jnp.bfloat16),
        compiler_params=pltpu.CompilerParams(vmem_limit_bytes=32 * 2**20),
        cost_estimate=BRIEF,
        name="project",
    )(y, normed, *pieces)


def partial_kernel(where_ref, own_ref, after_ref, dq_ref, x_ref, inv_ref, gain_in_ref, *refs):
    *pieces, out_ref, gain_ref = refs
    core, y = where_ref[1], where_ref[2]
    rows = pl.ds(pl.multiple_of(where_ref[0] * TOK, TOK), TOK)
    grad_kv = (own_ref[rows, :] + after_ref[rows, :].astype(jnp.float32)).astype(jnp.bfloat16)
    inv = inv_ref[rows, :]
    for first, piece in zip(piece_columns(y, pieces), pieces):
        count = piece.shape[0]
        cols = pl.ds(pl.multiple_of(first, count), count)
        grad = lax.dot_general(
            grad_kv, piece[...], (((1,), (1,)), ((), ())), preferred_element_type=jnp.float32
        )
        dq = dq_ref[rows, pl.ds(pl.multiple_of(first % HALF, count), count)]
        grad += jnp.where(first // HALF == core, dq, 0.0)
        out_ref[:, cols] = grad.astype(out_ref.dtype)
        scaled = x_ref[rows, cols].astype(jnp.float32) * inv
        gain_ref[:, cols] = gain_in_ref[:, cols] + jnp.sum(grad * scaled, axis=0, keepdims=True)


def partial_grad(where, own, after, dq, x, inv_rms, gain_grad, pieces, kind):
    features = x.shape[1]
    return pl.pallas_call(
        partial_kernel,
        in_specs=[SCALARS] + [WHOLE] * (6 + len(pieces)),
        out_specs=[WHOLE, WHOLE],
        out_shape=[
            jax.ShapeDtypeStruct((TOK, features), kind),
            jax.ShapeDtypeStruct((1, features), jnp.float32),
        ],
        compiler_params=pltpu.CompilerParams(vmem_limit_bytes=40 * 2**20),
        cost_estimate=BRIEF,
        name="partial_grad",
    )(where, own, after, dq, x, inv_rms, gain_grad, *pieces)


def input_grad_kernel(own_ref, other_ref, x_ref, inv_ref, upper_ref, gain_ref, up_ref, down_ref, grad_ref):
    features = x_ref.shape[1]
    width = 512
    blocks = [slice(at, at + width) for at in range(0, features, width)]
    inv_rms = inv_ref[...]
    inner = jnp.zeros((TOK, 1), jnp.float32)
    for cols in blocks:
        grad = (own_ref[:, cols] + other_ref[:, cols].astype(jnp.float32)) * gain_ref[:, cols]
        scaled = x_ref[:, cols].astype(jnp.float32) * inv_rms
        inner += jnp.sum(grad * scaled, axis=-1, keepdims=True)
        grad_ref[:, cols] = grad
    mean = inner * (1.0 / features)
    for first, ref in ((0, up_ref), (TOK // 2, down_ref)):
        rows = slice(first, first + TOK // 2)
        inv = inv_rms[rows]
        for cols in blocks:
            scaled = x_ref[rows, cols].astype(jnp.float32) * inv
            out = inv * (grad_ref[rows, cols] - scaled * mean[rows])
            ref[:, cols] = (out + upper_ref[rows, cols].astype(jnp.float32)).astype(jnp.bfloat16)


def input_grad(own, other, x, inv_rms, upper, gain_row):
    features = x.shape[1]
    return pl.pallas_call(
        input_grad_kernel,
        in_specs=[WHOLE] * 6,
        out_specs=[WHOLE, WHOLE],
        out_shape=[jax.ShapeDtypeStruct((TOK // 2, features), jnp.bfloat16)] * 2,
        scratch_shapes=[pltpu.VMEM((TOK, features), jnp.float32)],
        compiler_params=pltpu.CompilerParams(vmem_limit_bytes=32 * 2**20),
        cost_estimate=BRIEF,
        name="input_grad",
    )(own, other, x, inv_rms, upper, gain_row)


def body(section_in, back_in, upstream, gains, kv_weight):
    index = lax.axis_index("ctx").astype(jnp.int32)
    core, z_lo, y = index % CORES, (index // CORES) % Z_LO, index // (CORES * Z_LO)
    place, y_place = index.reshape(1), y.reshape(1)
    x_back, upper_in = back_in[0], upstream[0]

    chip_x_fwd = chip_rows(section_in[0], swap(section_in[0]), core)
    run = gather_run(kv_weight[0], core, z_lo)
    later_x, later_upper, run = lax.optimization_barrier((x_back, upper_in, run))
    chip_x_back = chip_rows(x_back, swap(later_x), core)
    chip_back, inv_back = norm_forward(chip_x_back, gains)
    chip_fwd, inv_fwd = norm_forward(chip_x_fwd, gains)
    chip_upper = chip_columns(later_upper, core)

    crossing = columns_of(chip_x_fwd, core)
    norms = direct(
        jnp.concatenate([columns_of(gains, core), inv_fwd.reshape(1, CHIP_TOK)], axis=1), 1
    )

    def first_out(after):
        part, _ = lax.optimization_barrier((crossing[:TOK], after))
        return halfway(part, 1)

    def second_out(after):
        part, _ = lax.optimization_barrier((crossing[TOK:], after))
        return halfway(part, -1)

    def first_in(part):
        return arrive(part, 1, 1)

    pieces, first_here, second_half = gather_weight(run, (first_out, second_out, first_in))
    chip_back, chip_fwd, chip_upper, norms = lax.optimization_barrier(
        (chip_back, chip_fwd, chip_upper, norms)
    )
    second_here = arrive(second_half, -1, 1)

    kv_back = project(y_place, chip_back, pieces)
    before = to_next_chip(kv_back)
    kv_here = direct(project(y_place, chip_fwd, pieces), 1)

    dq, grad_before, grad_own = backward_attention(place, chip_back, chip_upper, before, kv_back)
    after, kv_here, second_here = lax.optimization_barrier(
        (to_chip_before(grad_before), kv_here, second_here)
    )

    def partial(row, gain_grad, kind):
        where = jnp.stack([row, core, y])
        return partial_grad(
            where, grad_own, after, dq, chip_x_back, inv_back, gain_grad, pieces, kind
        )

    away, gain_grad = partial(1 - core, jnp.zeros_like(gains), jnp.bfloat16)
    away = swap(away)
    home, gain_grad = partial(core, gain_grad, jnp.float32)
    gain_grad = gain_grad + over_ctx(gain_grad, lambda y, z, c: (y, z ^ 1, c))
    gain_grad = gain_grad + over_ctx(gain_grad, lambda y, z, c: (y, z ^ 2, c))
    inv_own = lax.dynamic_slice_in_dim(inv_back, core * TOK, TOK, 0)
    up, down = input_grad(home, away, x_back, inv_own, upper_in, gains)
    up, gain_grad = lax.optimization_barrier((up, gain_grad))
    up_half, down_half = halfway(up, 1), halfway(down, -1)

    gain_grad = gain_grad + swap(gain_grad)
    up_half, down_half, gain_grad = lax.optimization_barrier((up_half, down_half, gain_grad))
    next_grad = jnp.concatenate([arrive(up_half, 1, -1), arrive(down_half, -1, -1)], axis=0)
    rings = [[(y * Z_LO + z) * CORES + c for y in range(Y)] for z in range(Z_LO) for c in range(CORES)]
    gathered = lax.all_gather(gain_grad, "ctx", axis_index_groups=rings, axis=0, tiled=True)
    gain_total = jnp.sum(gathered, axis=0, keepdims=True)

    kv_here, norms, _ = lax.optimization_barrier((kv_here, norms, up))
    out = forward_attention(
        place,
        first_here,
        second_here,
        norms[:, HALF:].reshape(CHIP_TOK, 1),
        norms[:, :HALF],
        to_next_chip(kv_here),
        kv_here,
    )
    first, second = out[:TOK], out[TOK:]
    mine = jnp.where(core == 0, first, second)
    other = swap(jnp.where(core == 0, second, first))
    next_in = jnp.concatenate(
        [jnp.where(core == 0, mine, other), jnp.where(core == 0, other, mine)], axis=1
    )
    return (next_in[None], next_grad[None], gain_total)


def solution(mesh):
    in_specs = (
        P("section", "ctx", None),
        P("section", "ctx", None),
        P("section", "ctx", None),
        P("section", None),
        P("section", "ctx", None),
    )
    out_specs = (P("section", "ctx", None), P("section", "ctx", None), P("section", None))
    return jax.shard_map(body, mesh=mesh, in_specs=in_specs, out_specs=out_specs, check_vma=False)
```

```python
import functools

import jax
import jax.numpy as jnp
from jax import lax
from jax.experimental import pallas as pl
from jax.experimental.pallas import tpu as pltpu
from jax.sharding import PartitionSpec as P

HD = 128
STEPS = 2
EPSILON = 1e-05
GROUP = 8
KVH = 4
TOK = 128
SPAN = (STEPS + 1) * TOK

X, Z_HI, Y, Z_LO, CORES = 4, 2, 8, 4, 2
Z = Z_HI * Z_LO
CHIPS = Y * Z_LO
CTX = Y * Z_LO * CORES

HEADS = KVH // CORES
CHIP_TOK = CORES * TOK
HALF = HEADS * GROUP * HD

SCALE = HD ** (-0.5)
LOG2E = 1.4426950408889634


def ctx_pairs(move):
    pairs = []
    for c in range(CTX):
        target = move(c // (Z_LO * CORES), (c // CORES) % Z_LO, c % CORES)
        if target is not None:
            y, z_lo, core = target
            pairs.append((c, (y * Z_LO + z_lo) * CORES + core))
    return pairs


def over_ctx(value, move):
    return lax.ppermute(value, "ctx", ctx_pairs(move))


def grid_pairs(move):
    pairs = []
    for x in range(X):
        for z in range(Z):
            for core in range(CORES):
                new_x, new_z = move(x, z, core)
                new_x, new_z = (new_x % X, new_z % Z)
                for y in range(Y):
                    source = (x * Z_HI + z // Z_LO) * CTX + (y * Z_LO + z % Z_LO) * CORES + core
                    target = (new_x * Z_HI + new_z // Z_LO) * CTX + (y * Z_LO + new_z % Z_LO) * CORES + core
                    pairs.append((source, target))
    return pairs


def over_grid(value, move):
    return lax.ppermute(value, ("section", "ctx"), grid_pairs(move))


WAY = (2, -2)


def halfway(value):
    return over_grid(value, lambda x, z, core: (x, z + WAY[core]))


def arrive(value, distance):
    def move(x, z, core):
        z_hi = ((z - WAY[core]) % Z) // Z_LO
        cross = (1 if z_hi == Z_HI - 1 else 0) if distance == 1 else (-1 if z_hi == 0 else 0)
        return (x + cross, z + WAY[core])

    return over_grid(value, move)


def direct(value, distance):
    peers = Z_HI * X
    return lax.ppermute(value, "section", [(i, (i + distance) % peers) for i in range(peers)])


def norm_forward(section_x, gain_row):
    values = section_x.astype(jnp.float32)
    inv_rms = lax.rsqrt(jnp.mean(values * values, axis=-1, keepdims=True) + EPSILON)
    return (values * inv_rms * gain_row).astype(jnp.bfloat16), inv_rms


def by_head(kv_columns):
    parts = []
    for head in range(KVH):
        parts.append(kv_columns[:, head * HD : (head + 1) * HD])
        parts.append(kv_columns[:, (KVH + head) * HD : (KVH + head + 1) * HD])
    return jnp.concatenate(parts, axis=1)


def gather_run(own_rows, core, z_lo):
    half = own_rows.shape[1] // 2
    columns = by_head(own_rows)
    low, high = columns[:, :half], columns[:, half:]
    keep = jnp.where(core == 0, low, high)
    received = swap(jnp.where(core == 0, high, low))
    chip = chip_rows(keep, received, core)
    rows = chip.shape[0]
    pieces = [chip]
    for step in range(1, Z_LO):
        pieces.append(over_ctx(chip, lambda y, z, c, step=step: (y, (z + step) % Z_LO, c)))
    back = pieces[::-1]
    return lax.dynamic_slice_in_dim(
        jnp.concatenate(back + back[:-1], axis=0), (Z_LO - 1 - z_lo) * rows, Z_LO * rows, 0
    )


def gather_weight(run, crossing):
    def up(piece):
        return over_ctx(piece, lambda y, z, c: ((y + 1) % Y, z, c))

    def down(piece):
        return over_ctx(piece, lambda y, z, c: ((y - 1) % Y, z, c))

    crossing = halfway(crossing)
    rising, falling = [up(run)], [down(run)]
    rising.append(up(rising[0]))
    falling.append(down(falling[0]))
    rising[1], falling[1], crossing = lax.optimization_barrier((rising[1], falling[1], crossing))
    crossing = arrive(crossing, 1)
    rising.append(up(rising[1]))
    falling.append(down(falling[1]))
    middle = run.shape[0] // 2
    rising.append(up(rising[2][:middle]))
    falling.append(down(falling[2][middle:]))
    rising[3], falling[3], crossing = lax.optimization_barrier((rising[3], falling[3], crossing))
    return [run, *falling[:3], rising[3], falling[3], *rising[:3][::-1]], crossing


def swap(value):
    return over_ctx(value, lambda y, z, c: (y, z, 1 - c))


def chip_rows(own, partner, core):
    return jnp.concatenate(
        [jnp.where(core == 0, own, partner), jnp.where(core == 0, partner, own)], axis=0
    )


def to_next_chip(value):
    pairs = [(i, i + CORES) for i in range(CTX - CORES)]
    return lax.ppermute(value, "ctx", pairs)


def to_chip_before(value):
    pairs = [(i, i - CORES) for i in range(CORES, CTX)]
    return lax.ppermute(value, "ctx", pairs)


def columns_of(value, core):
    return lax.dynamic_slice_in_dim(value, core * HALF, HALF, 1)


def chip_columns(value, core):
    return chip_rows(columns_of(value, core), swap(columns_of(value, 1 - core)), core)


def stacked(ref, tokens):
    rows = slice(tokens * TOK, (tokens + 1) * TOK)
    return jnp.concatenate([ref[rows, g * HD : (g + 1) * HD] for g in range(GROUP)], axis=0)


def masked_scores(keys, queries, tokens, any_before):
    scores = lax.dot_general(
        keys, queries, (((1,), (1,)), ((), ())), preferred_element_type=jnp.float32
    )
    across = queries.shape[0]
    before = (STEPS - tokens) * TOK
    seen = lax.broadcasted_iota(jnp.int32, (TOK, across), 0)
    query = lax.broadcasted_iota(jnp.int32, (TOK, across), 1) % TOK
    parts = [jnp.where(any_before, scores[:before], -1e30)]
    if tokens:
        parts.append(scores[before : STEPS * TOK])
    parts.append(jnp.where(seen <= query, scores[STEPS * TOK :], -1e30))
    return jnp.concatenate(parts, axis=0)


PAIR = 2
WIDE = GROUP * HD

BRIEF = pl.CostEstimate(flops=1000, bytes_accessed=1000, transcendentals=0)


def forward_kernel(index_ref, x_ref, inv_ref, gain_ref, before_ref, own_ref, out_ref):
    any_before = index_ref[0] >= CORES
    keys = jnp.concatenate([before_ref[:, :HD], own_ref[:, :HD]], axis=0)
    values = jnp.concatenate([before_ref[:, HD:], own_ref[:, HD:]], axis=0)
    values_t = values.astype(jnp.float32).T.astype(jnp.bfloat16)
    for tokens in range(CORES):
        span = slice(tokens * TOK, tokens * TOK + SPAN)
        rows = slice(tokens * TOK, (tokens + 1) * TOK)
        terms = inv_ref[rows, :].astype(jnp.float32)
        inv = terms[:, 0:1] + terms[:, 1:2] + terms[:, 2:3]
        for pair in range(GROUP // PAIR):
            cols = [
                slice(g * HD, (g + 1) * HD) for g in range(pair * PAIR, (pair + 1) * PAIR)
            ]
            x = [x_ref[rows, at].astype(jnp.float32) for at in cols]
            queries = jnp.concatenate(
                [(part * inv * gain_ref[:, at]).astype(jnp.bfloat16) for part, at in zip(x, cols)],
                axis=0,
            )
            scores = masked_scores(keys[span], queries, tokens, any_before)
            top = jnp.max(scores, axis=0, keepdims=True)
            terms = jnp.exp2((scores - top) * (SCALE * LOG2E))
            total = jnp.sum(terms, axis=0, keepdims=True)
            attended = jnp.dot(
                values_t[:, span], terms.astype(jnp.bfloat16), preferred_element_type=jnp.float32
            ) * (1.0 / total)
            for g, at in enumerate(cols):
                out = attended[:, g * TOK : (g + 1) * TOK].T + x[g]
                out_ref[rows, at] = out.astype(jnp.bfloat16)


def forward_attention(index, crossed, gain, before, own):
    heads = pl.BlockSpec((CHIP_TOK, WIDE), lambda h, index: (0, h))
    kv = pl.BlockSpec((CHIP_TOK, 2 * HD), lambda h, index: (0, h))
    return pl.pallas_call(
        forward_kernel,
        grid_spec=pltpu.PrefetchScalarGridSpec(
            num_scalar_prefetch=1,
            grid=(HEADS,),
            in_specs=[
                heads,
                pl.BlockSpec((CHIP_TOK, HD), lambda h, index: (0, 2 * HEADS)),
                pl.BlockSpec((1, WIDE), lambda h, index: (0, h)),
                kv,
                kv,
            ],
            out_specs=heads,
        ),
        out_shape=jax.ShapeDtypeStruct((CHIP_TOK, HALF), jnp.bfloat16),
        compiler_params=pltpu.CompilerParams(vmem_limit_bytes=20 * 2**20),
        cost_estimate=BRIEF,
        name="forward_attention",
    )(index, crossed, own, gain, before, own)


def backward_kernel(
    index_ref, normed_ref, upper_ref, before_ref, own_ref, dq_ref, grad_before_ref, grad_own_ref,
    probs_ref, dlog_ref,
):
    any_before = index_ref[0] >= CORES
    keys = jnp.concatenate([before_ref[:, :HD], own_ref[:, :HD]], axis=0)
    values = jnp.concatenate([before_ref[:, HD:], own_ref[:, HD:]], axis=0)
    keys_t = keys.astype(jnp.float32).T.astype(jnp.bfloat16)
    queries = [stacked(normed_ref, tokens) for tokens in range(CORES)]
    uppers = [stacked(upper_ref, tokens) for tokens in range(CORES)]
    for tokens in range(CORES):
        span = slice(tokens * TOK, tokens * TOK + SPAN)
        for pair in range(GROUP // PAIR):
            these = slice(pair * PAIR * TOK, (pair + 1) * PAIR * TOK)
            scores = masked_scores(keys[span], queries[tokens][these], tokens, any_before)
            grad_probs = lax.dot_general(
                values[span],
                uppers[tokens][these],
                (((1,), (1,)), ((), ())),
                preferred_element_type=jnp.float32,
            )
            top = jnp.max(scores, axis=0, keepdims=True)
            terms = jnp.exp2((scores - top) * (SCALE * LOG2E))
            inverse = 1.0 / jnp.sum(terms, axis=0, keepdims=True)
            row_dot = jnp.sum(terms * grad_probs, axis=0, keepdims=True) * inverse
            probs = terms * inverse
            cols = slice(tokens * WIDE + these.start, tokens * WIDE + these.stop)
            probs_ref[span, cols] = probs.astype(jnp.bfloat16)
            dlog_ref[span, cols] = (probs * ((grad_probs - row_dot) * SCALE)).astype(jnp.bfloat16)
        dlogits = dlog_ref[span, tokens * WIDE : (tokens + 1) * WIDE]
        grad_query = jnp.dot(keys_t[:, span], dlogits, preferred_element_type=jnp.float32)
        rows = slice(tokens * TOK, (tokens + 1) * TOK)
        for g in range(GROUP):
            dq_ref[rows, g * HD : (g + 1) * HD] = grad_query[:, g * TOK : (g + 1) * TOK].T
    for left, factors, first in ((dlog_ref, queries, 0), (probs_ref, uppers, HD)):
        cols = slice(first, first + HD)

        def product(rows, tokens, last):
            factor = jnp.concatenate(factors[tokens:last], axis=0)
            return jnp.dot(
                left[rows, tokens * WIDE : last * WIDE], factor, preferred_element_type=jnp.float32
            )

        middle = product(slice(TOK, 3 * TOK), 0, 2)
        grad_before_ref[:TOK, cols] = product(slice(0, TOK), 0, 1).astype(jnp.bfloat16)
        grad_before_ref[TOK:, cols] = middle[:TOK].astype(jnp.bfloat16)
        grad_own_ref[:TOK, cols] = middle[TOK:]
        grad_own_ref[TOK:, cols] = product(slice(3 * TOK, 4 * TOK), 1, 2)


def backward_attention(index, normed, upper, before, own):
    kv = pl.BlockSpec((CHIP_TOK, 2 * HD), lambda h, index: (0, h))
    heads = pl.BlockSpec((CHIP_TOK, WIDE), lambda h, index: (0, h))
    return pl.pallas_call(
        backward_kernel,
        grid_spec=pltpu.PrefetchScalarGridSpec(
            num_scalar_prefetch=1,
            grid=(HEADS,),
            in_specs=[
                pl.BlockSpec((CHIP_TOK, WIDE), lambda h, index: (0, (index[0] % CORES) * HEADS + h)),
                heads,
                kv,
                kv,
            ],
            out_specs=[heads, kv, kv],
            scratch_shapes=[
                pltpu.VMEM((4 * TOK, CORES * WIDE), jnp.bfloat16),
                pltpu.VMEM((4 * TOK, CORES * WIDE), jnp.bfloat16),
            ],
        ),
        out_shape=[
            jax.ShapeDtypeStruct((CHIP_TOK, HALF), jnp.float32),
            jax.ShapeDtypeStruct(before.shape, jnp.bfloat16),
            jax.ShapeDtypeStruct(own.shape, jnp.float32),
        ],
        compiler_params=pltpu.CompilerParams(vmem_limit_bytes=24 * 2**20),
        cost_estimate=BRIEF,
        name="backward_attention",
    )(index, normed, upper, before, own)


def piece_columns(y, pieces):
    firsts, at = [], 0
    block = pieces[0].shape[0]
    for piece in pieces:
        firsts.append(pl.multiple_of(((y + at // block) % Y) * block, block) + at % block)
        at += piece.shape[0]
    return firsts


def project_kernel(y_ref, normed_ref, beside_ref, *refs):
    *pieces, out_ref = refs
    width = pieces[0].shape[1]
    total = jnp.zeros((normed_ref.shape[0], width), jnp.float32)
    for first, piece in zip(piece_columns(y_ref[0], pieces), pieces):
        rows = piece.shape[0]
        part = normed_ref[:, pl.ds(pl.multiple_of(first, rows), rows)]
        total += jnp.dot(part, piece[...], preferred_element_type=jnp.float32)
    out_ref[:, :width] = total.astype(out_ref.dtype)
    if out_ref.shape[1] > width:
        out_ref[:, width:] = beside_ref[...]


SCALARS = pl.BlockSpec(memory_space=pltpu.SMEM)
WHOLE = pl.BlockSpec(memory_space=pltpu.VMEM)


def project(y, normed, pieces, beside, with_beside):
    width = pieces[0].shape[1] + (beside.shape[1] if with_beside else 0)
    return pl.pallas_call(
        project_kernel,
        in_specs=[SCALARS] + [WHOLE] * (2 + len(pieces)),
        out_specs=WHOLE,
        out_shape=jax.ShapeDtypeStruct((normed.shape[0], width), jnp.bfloat16),
        compiler_params=pltpu.CompilerParams(vmem_limit_bytes=16 * 2**20),
        cost_estimate=BRIEF,
        name="project",
    )(y, normed, beside, *pieces)


def partial_kernel(where_ref, own_ref, after_ref, dq_ref, *refs):
    *pieces, out_ref = refs
    core, y = where_ref[1], where_ref[2]
    rows = pl.ds(pl.multiple_of(where_ref[0] * TOK, TOK), TOK)
    grad_kv = (own_ref[rows, :] + after_ref[rows, :].astype(jnp.float32)).astype(jnp.bfloat16)
    for first, piece in zip(piece_columns(y, pieces), pieces):
        count = piece.shape[0]
        grad = lax.dot_general(
            grad_kv, piece[...], (((1,), (1,)), ((), ())), preferred_element_type=jnp.float32
        )
        dq = dq_ref[rows, pl.ds(pl.multiple_of(first % HALF, count), count)]
        grad += jnp.where(first // HALF == core, dq, 0.0)
        out_ref[:, pl.ds(pl.multiple_of(first, count), count)] = grad.astype(out_ref.dtype)


def partial_grad(where, own, after, dq, pieces, kind):
    return pl.pallas_call(
        partial_kernel,
        in_specs=[SCALARS] + [WHOLE] * (3 + len(pieces)),
        out_specs=WHOLE,
        out_shape=jax.ShapeDtypeStruct((TOK, CORES * HALF), kind),
        compiler_params=pltpu.CompilerParams(vmem_limit_bytes=20 * 2**20),
        cost_estimate=BRIEF,
        name="partial_grad",
    )(where, own, after, dq, *pieces)


def input_grad_kernel(own_ref, other_ref, x_ref, upper_ref, gain_ref, out_ref, gain_grad_ref, grad_ref):
    features = x_ref.shape[1]
    width = 512
    blocks = [slice(at, at + width) for at in range(0, features, width)]
    squares = jnp.zeros((TOK, 1), jnp.float32)
    for cols in blocks:
        part = x_ref[:, cols].astype(jnp.float32)
        squares += jnp.sum(part * part, axis=-1, keepdims=True)
    inv_rms = lax.rsqrt(squares / features + EPSILON)
    inner = jnp.zeros((TOK, 1), jnp.float32)
    for cols in blocks:
        grad = own_ref[:, cols] + other_ref[:, cols].astype(jnp.float32)
        scaled = x_ref[:, cols].astype(jnp.float32) * inv_rms
        product = grad * scaled
        gain_grad_ref[:, cols] = jnp.sum(product, axis=0, keepdims=True)
        gain = gain_ref[:, cols]
        inner += jnp.sum(product * gain, axis=-1, keepdims=True)
        grad_ref[:, cols] = grad * gain
    mean = inner * (1.0 / features)
    for cols in blocks:
        scaled = x_ref[:, cols].astype(jnp.float32) * inv_rms
        out = inv_rms * (grad_ref[:, cols] - scaled * mean)
        out_ref[:, cols] = (out + upper_ref[:, cols].astype(jnp.float32)).astype(jnp.bfloat16)


def input_grad(own, other, x, upper, gain_row):
    features = x.shape[1]
    return pl.pallas_call(
        input_grad_kernel,
        in_specs=[WHOLE] * 5,
        out_specs=[WHOLE, WHOLE],
        out_shape=[
            jax.ShapeDtypeStruct((TOK, features), jnp.bfloat16),
            jax.ShapeDtypeStruct((1, features), jnp.float32),
        ],
        scratch_shapes=[pltpu.VMEM((TOK, features), jnp.float32)],
        compiler_params=pltpu.CompilerParams(vmem_limit_bytes=16 * 2**20),
        cost_estimate=BRIEF,
        name="input_grad",
    )(own, other, x, upper, gain_row)


def in_three(value):
    terms = []
    for _ in range(3):
        term = lax.reduce_precision(value, 8, 7)
        terms.append(term.astype(jnp.bfloat16))
        value = value - term
    blank = jnp.zeros((value.shape[0], HD - len(terms)), jnp.bfloat16)
    return jnp.concatenate(terms + [blank], axis=1)


def body(section_in, back_in, upstream, gains, kv_weight):
    index = lax.axis_index("ctx").astype(jnp.int32)
    core, z_lo, y = index % CORES, (index // CORES) % Z_LO, index // (CORES * Z_LO)
    place, y_place = index.reshape(1), y.reshape(1)
    x_back, upper_in = back_in[0], upstream[0]

    chip_x_fwd = chip_rows(section_in[0], swap(section_in[0]), core)
    crossing = columns_of(chip_x_fwd, core)
    run = gather_run(kv_weight[0], core, z_lo)
    gain_here = direct(columns_of(gains, core), 1)
    later_x, later_upper, run, gain_here, crossing = lax.optimization_barrier(
        (x_back, upper_in, run, gain_here, crossing)
    )
    chip_x_back = chip_rows(x_back, swap(later_x), core)
    chip_back, _ = norm_forward(chip_x_back, gains)
    chip_fwd, inv_fwd = norm_forward(chip_x_fwd, gains)
    chip_upper = chip_columns(later_upper, core)

    pieces, crossed = gather_weight(run, crossing)
    chip_back, chip_fwd, chip_upper, norms = lax.optimization_barrier(
        (chip_back, chip_fwd, chip_upper, in_three(inv_fwd))
    )

    kv_back = project(y_place, chip_back, pieces, norms, False)
    before = to_next_chip(kv_back)
    kv_here = direct(project(y_place, chip_fwd, pieces, norms, True), 1)

    dq, grad_before, grad_own = backward_attention(place, chip_back, chip_upper, before, kv_back)
    after, kv_here = lax.optimization_barrier((to_chip_before(grad_before), kv_here))

    def partial(row, kind):
        return partial_grad(jnp.stack([row, core, y]), grad_own, after, dq, pieces, kind)

    away = swap(partial(1 - core, jnp.bfloat16))
    home = partial(core, jnp.float32)
    grad_in, gain_grad = input_grad(home, away, x_back, upper_in, gains)
    half_sent = halfway(grad_in)

    kv_here, gain_here, _ = lax.optimization_barrier((kv_here, gain_here, grad_in))
    out = forward_attention(place, crossed, gain_here, to_next_chip(kv_here), kv_here)
    first, second = out[:TOK], out[TOK:]
    mine = jnp.where(core == 0, first, second)
    other = swap(jnp.where(core == 0, second, first))
    next_in = jnp.concatenate(
        [jnp.where(core == 0, mine, other), jnp.where(core == 0, other, mine)], axis=1
    )

    gain_grad = gain_grad + swap(gain_grad)
    half_sent, gain_grad = lax.optimization_barrier((half_sent, gain_grad))
    next_grad = arrive(half_sent, -1)
    for bit in (1, 2, 4):
        gain_grad = gain_grad + over_ctx(gain_grad, lambda y, z, c: (y ^ bit, z, c))
    next_grad, gain_grad = lax.optimization_barrier((next_grad, gain_grad))
    for bit in (1, 2):
        gain_grad = gain_grad + over_ctx(gain_grad, lambda y, z, c: (y, z ^ bit, c))
    return (next_in[None], next_grad[None], gain_grad)


def solution(mesh):
    in_specs = (
        P("section", "ctx", None),
        P("section", "ctx", None),
        P("section", "ctx", None),
        P("section", None),
        P("section", "ctx", None),
    )
    out_specs = (P("section", "ctx", None), P("section", "ctx", None), P("section", None))
    return jax.shard_map(body, mesh=mesh, in_specs=in_specs, out_specs=out_specs, check_vma=False)
```

```python
import functools

import jax
import jax.numpy as jnp
from jax import lax
from jax.experimental import pallas as pl
from jax.experimental.pallas import tpu as pltpu
from jax.sharding import PartitionSpec as P

HD = 128
STEPS = 2
EPSILON = 1e-05
GROUP = 8
KVH = 4
TOK = 128
SPAN = (STEPS + 1) * TOK

X, Z_HI, Y, Z_LO, CORES = 4, 2, 8, 4, 2
Z = Z_HI * Z_LO
CHIPS = Y * Z_LO
CTX = Y * Z_LO * CORES

HEADS = KVH // CORES
CHIP_TOK = CORES * TOK
HALF = HEADS * GROUP * HD

SCALE = HD ** (-0.5)
LOG2E = 1.4426950408889634


def ctx_pairs(move):
    pairs = []
    for c in range(CTX):
        target = move(c // (Z_LO * CORES), (c // CORES) % Z_LO, c % CORES)
        if target is not None:
            y, z_lo, core = target
            pairs.append((c, (y * Z_LO + z_lo) * CORES + core))
    return pairs


def over_ctx(value, move):
    return lax.ppermute(value, "ctx", ctx_pairs(move))


def grid_pairs(move):
    pairs = []
    for x in range(X):
        for z in range(Z):
            for core in range(CORES):
                new_x, new_z = move(x, z, core)
                new_x, new_z = (new_x % X, new_z % Z)
                for y in range(Y):
                    source = (x * Z_HI + z // Z_LO) * CTX + (y * Z_LO + z % Z_LO) * CORES + core
                    target = (new_x * Z_HI + new_z // Z_LO) * CTX + (y * Z_LO + new_z % Z_LO) * CORES + core
                    pairs.append((source, target))
    return pairs


def over_grid(value, move):
    return lax.ppermute(value, ("section", "ctx"), grid_pairs(move))


UP, DOWN, SPLIT = (2, 2), (-2, -2), (2, -2)


def halfway(value, way):
    return over_grid(value, lambda x, z, core: (x, z + way[core]))


def arrive(value, way, distance):
    def move(x, z, core):
        z_hi = ((z - way[core]) % Z) // Z_LO
        cross = (1 if z_hi == Z_HI - 1 else 0) if distance == 1 else (-1 if z_hi == 0 else 0)
        return (x + cross, z + way[core])

    return over_grid(value, move)


def direct(value, distance):
    peers = Z_HI * X
    return lax.ppermute(value, "section", [(i, (i + distance) % peers) for i in range(peers)])


def norm_forward(section_x, gain_row):
    values = section_x.astype(jnp.float32)
    inv_rms = lax.rsqrt(jnp.mean(values * values, axis=-1, keepdims=True) + EPSILON)
    return (values * inv_rms * gain_row).astype(jnp.bfloat16), inv_rms


def by_head(kv_columns):
    parts = []
    for head in range(KVH):
        parts.append(kv_columns[:, head * HD : (head + 1) * HD])
        parts.append(kv_columns[:, (KVH + head) * HD : (KVH + head + 1) * HD])
    return jnp.concatenate(parts, axis=1)


def gather_run(own_rows, core, z_lo, first):
    half = own_rows.shape[1] // 2
    columns = by_head(own_rows)
    low, high = columns[:, :half], columns[:, half:]
    keep = jnp.where(core == 0, low, high)
    received, first = lax.optimization_barrier((swap(jnp.where(core == 0, high, low)), first))
    chip = chip_rows(keep, received, core)
    rows = chip.shape[0]
    pieces = [chip]
    for step in range(1, Z_LO):
        pieces.append(over_ctx(chip, lambda y, z, c, step=step: (y, (z + step) % Z_LO, c)))
    back = pieces[::-1]
    run = lax.dynamic_slice_in_dim(
        jnp.concatenate(back + back[:-1], axis=0), (Z_LO - 1 - z_lo) * rows, Z_LO * rows, 0
    )
    return run, first


def gather_weight(run, crossing):
    def up(piece):
        return over_ctx(piece, lambda y, z, c: ((y + 1) % Y, z, c))

    def down(piece):
        return over_ctx(piece, lambda y, z, c: ((y - 1) % Y, z, c))

    crossing = halfway(crossing, SPLIT)
    rising, falling = [up(run)], [down(run)]
    rising.append(up(rising[0]))
    falling.append(down(falling[0]))
    rising[1], falling[1], crossing = lax.optimization_barrier((rising[1], falling[1], crossing))
    rising.append(up(rising[1]))
    falling.append(down(falling[1]))
    middle = run.shape[0] // 2
    rising.append(up(rising[2][:middle]))
    falling.append(down(falling[2][middle:]))
    pieces = [run, *falling[:3], rising[3], falling[3], *rising[:3][::-1]]
    return pieces, arrive(crossing, SPLIT, 1)


def swap(value):
    return over_ctx(value, lambda y, z, c: (y, z, 1 - c))


def chip_rows(own, partner, core):
    return jnp.concatenate(
        [jnp.where(core == 0, own, partner), jnp.where(core == 0, partner, own)], axis=0
    )


def to_next_chip(value):
    pairs = [(i, i + CORES) for i in range(CTX - CORES)]
    return lax.ppermute(value, "ctx", pairs)


def to_chip_before(value):
    pairs = [(i, i - CORES) for i in range(CORES, CTX)]
    return lax.ppermute(value, "ctx", pairs)


def columns_of(value, core):
    return lax.dynamic_slice_in_dim(value, core * HALF, HALF, 1)


def chip_columns(value, core):
    return chip_rows(columns_of(value, core), swap(columns_of(value, 1 - core)), core)


def stacked(ref, tokens):
    rows = slice(tokens * TOK, (tokens + 1) * TOK)
    return jnp.concatenate([ref[rows, g * HD : (g + 1) * HD] for g in range(GROUP)], axis=0)


def masked_scores(keys, queries, tokens, any_before):
    scores = lax.dot_general(
        keys, queries, (((1,), (1,)), ((), ())), preferred_element_type=jnp.float32
    )
    across = queries.shape[0]
    before = (STEPS - tokens) * TOK
    seen = lax.broadcasted_iota(jnp.int32, (TOK, across), 0)
    query = lax.broadcasted_iota(jnp.int32, (TOK, across), 1) % TOK
    parts = [jnp.where(any_before, scores[:before], -1e30)]
    if tokens:
        parts.append(scores[before : STEPS * TOK])
    parts.append(jnp.where(seen <= query, scores[STEPS * TOK :], -1e30))
    return jnp.concatenate(parts, axis=0)


PAIR = 2
WIDE = GROUP * HD

BRIEF = pl.CostEstimate(flops=1000, bytes_accessed=1000, transcendentals=0)


def forward_kernel(index_ref, x_ref, inv_ref, gain_ref, before_ref, own_ref, out_ref):
    any_before = index_ref[0] >= CORES
    keys = jnp.concatenate([before_ref[:, :HD], own_ref[:, :HD]], axis=0)
    values = jnp.concatenate([before_ref[:, HD:], own_ref[:, HD:]], axis=0)
    values_t = values.astype(jnp.float32).T.astype(jnp.bfloat16)
    for tokens in range(CORES):
        span = slice(tokens * TOK, tokens * TOK + SPAN)
        rows = slice(tokens * TOK, (tokens + 1) * TOK)
        terms = inv_ref[rows, :].astype(jnp.float32)
        inv = terms[:, 0:1] + terms[:, 1:2] + terms[:, 2:3]
        for pair in range(GROUP // PAIR):
            cols = [
                slice(g * HD, (g + 1) * HD) for g in range(pair * PAIR, (pair + 1) * PAIR)
            ]
            x = [x_ref[rows, at].astype(jnp.float32) for at in cols]
            queries = jnp.concatenate(
                [(part * inv * gain_ref[:, at]).astype(jnp.bfloat16) for part, at in zip(x, cols)],
                axis=0,
            )
            scores = masked_scores(keys[span], queries, tokens, any_before)
            top = jnp.max(scores, axis=0, keepdims=True)
            terms = jnp.exp2((scores - top) * (SCALE * LOG2E))
            total = jnp.sum(terms, axis=0, keepdims=True)
            attended = jnp.dot(
                values_t[:, span], terms.astype(jnp.bfloat16), preferred_element_type=jnp.float32
            ) * (1.0 / total)
            for g, at in enumerate(cols):
                out = attended[:, g * TOK : (g + 1) * TOK].T + x[g]
                out_ref[rows, at] = out.astype(jnp.bfloat16)


def forward_attention(index, crossed, gain, before, own):
    heads = pl.BlockSpec((CHIP_TOK, WIDE), lambda h, index: (0, h))
    kv = pl.BlockSpec((CHIP_TOK, 2 * HD), lambda h, index: (0, h))
    return pl.pallas_call(
        forward_kernel,
        grid_spec=pltpu.PrefetchScalarGridSpec(
            num_scalar_prefetch=1,
            grid=(HEADS,),
            in_specs=[
                heads,
                pl.BlockSpec((CHIP_TOK, HD), lambda h, index: (0, 2 * HEADS)),
                pl.BlockSpec((1, WIDE), lambda h, index: (0, h)),
                kv,
                kv,
            ],
            out_specs=heads,
        ),
        out_shape=jax.ShapeDtypeStruct((CHIP_TOK, HALF), jnp.bfloat16),
        compiler_params=pltpu.CompilerParams(vmem_limit_bytes=20 * 2**20),
        cost_estimate=BRIEF,
        name="forward_attention",
    )(index, crossed, own, gain, before, own)


def backward_kernel(
    index_ref, normed_ref, upper_ref, before_ref, own_ref, dq_ref, grad_before_ref, grad_own_ref,
    probs_ref, dlog_ref,
):
    any_before = index_ref[0] >= CORES
    keys = jnp.concatenate([before_ref[:, :HD], own_ref[:, :HD]], axis=0)
    values = jnp.concatenate([before_ref[:, HD:], own_ref[:, HD:]], axis=0)
    keys_t = keys.astype(jnp.float32).T.astype(jnp.bfloat16)
    queries = [stacked(normed_ref, tokens) for tokens in range(CORES)]
    uppers = [stacked(upper_ref, tokens) for tokens in range(CORES)]
    for tokens in range(CORES):
        span = slice(tokens * TOK, tokens * TOK + SPAN)
        for pair in range(GROUP // PAIR):
            these = slice(pair * PAIR * TOK, (pair + 1) * PAIR * TOK)
            scores = masked_scores(keys[span], queries[tokens][these], tokens, any_before)
            grad_probs = lax.dot_general(
                values[span],
                uppers[tokens][these],
                (((1,), (1,)), ((), ())),
                preferred_element_type=jnp.float32,
            )
            top = jnp.max(scores, axis=0, keepdims=True)
            terms = jnp.exp2((scores - top) * (SCALE * LOG2E))
            inverse = 1.0 / jnp.sum(terms, axis=0, keepdims=True)
            row_dot = jnp.sum(terms * grad_probs, axis=0, keepdims=True) * inverse
            probs = terms * inverse
            cols = slice(tokens * WIDE + these.start, tokens * WIDE + these.stop)
            probs_ref[span, cols] = probs.astype(jnp.bfloat16)
            dlog_ref[span, cols] = (probs * ((grad_probs - row_dot) * SCALE)).astype(jnp.bfloat16)
        dlogits = dlog_ref[span, tokens * WIDE : (tokens + 1) * WIDE]
        grad_query = jnp.dot(keys_t[:, span], dlogits, preferred_element_type=jnp.float32)
        rows = slice(tokens * TOK, (tokens + 1) * TOK)
        for g in range(GROUP):
            dq_ref[rows, g * HD : (g + 1) * HD] = grad_query[:, g * TOK : (g + 1) * TOK].T
    for left, factors, first in ((dlog_ref, queries, 0), (probs_ref, uppers, HD)):
        cols = slice(first, first + HD)

        def product(rows, tokens, last):
            factor = jnp.concatenate(factors[tokens:last], axis=0)
            return jnp.dot(
                left[rows, tokens * WIDE : last * WIDE], factor, preferred_element_type=jnp.float32
            )

        middle = product(slice(TOK, 3 * TOK), 0, 2)
        grad_before_ref[:TOK, cols] = product(slice(0, TOK), 0, 1).astype(jnp.bfloat16)
        grad_before_ref[TOK:, cols] = middle[:TOK].astype(jnp.bfloat16)
        grad_own_ref[:TOK, cols] = middle[TOK:]
        grad_own_ref[TOK:, cols] = product(slice(3 * TOK, 4 * TOK), 1, 2)


def backward_attention(index, normed, upper, before, own):
    kv = pl.BlockSpec((CHIP_TOK, 2 * HD), lambda h, index: (0, h))
    heads = pl.BlockSpec((CHIP_TOK, WIDE), lambda h, index: (0, h))
    return pl.pallas_call(
        backward_kernel,
        grid_spec=pltpu.PrefetchScalarGridSpec(
            num_scalar_prefetch=1,
            grid=(HEADS,),
            in_specs=[
                pl.BlockSpec((CHIP_TOK, WIDE), lambda h, index: (0, (index[0] % CORES) * HEADS + h)),
                heads,
                kv,
                kv,
            ],
            out_specs=[heads, kv, kv],
            scratch_shapes=[
                pltpu.VMEM((4 * TOK, CORES * WIDE), jnp.bfloat16),
                pltpu.VMEM((4 * TOK, CORES * WIDE), jnp.bfloat16),
            ],
        ),
        out_shape=[
            jax.ShapeDtypeStruct((CHIP_TOK, HALF), jnp.float32),
            jax.ShapeDtypeStruct(before.shape, jnp.bfloat16),
            jax.ShapeDtypeStruct(own.shape, jnp.float32),
        ],
        compiler_params=pltpu.CompilerParams(vmem_limit_bytes=24 * 2**20),
        cost_estimate=BRIEF,
        name="backward_attention",
    )(index, normed, upper, before, own)


def piece_columns(y, pieces):
    firsts, at = [], 0
    block = pieces[0].shape[0]
    for piece in pieces:
        firsts.append(pl.multiple_of(((y + at // block) % Y) * block, block) + at % block)
        at += piece.shape[0]
    return firsts


def project_kernel(y_ref, normed_ref, beside_ref, *refs):
    *pieces, out_ref = refs
    width = pieces[0].shape[1]
    total = jnp.zeros((normed_ref.shape[0], width), jnp.float32)
    for first, piece in zip(piece_columns(y_ref[0], pieces), pieces):
        rows = piece.shape[0]
        part = normed_ref[:, pl.ds(pl.multiple_of(first, rows), rows)]
        total += jnp.dot(part, piece[...], preferred_element_type=jnp.float32)
    out_ref[:, :width] = total.astype(out_ref.dtype)
    if out_ref.shape[1] > width:
        out_ref[:, width:] = beside_ref[...]


SCALARS = pl.BlockSpec(memory_space=pltpu.SMEM)
WHOLE = pl.BlockSpec(memory_space=pltpu.VMEM)


def project(y, normed, pieces, beside, with_beside):
    width = pieces[0].shape[1] + (beside.shape[1] if with_beside else 0)
    return pl.pallas_call(
        project_kernel,
        in_specs=[SCALARS] + [WHOLE] * (2 + len(pieces)),
        out_specs=WHOLE,
        out_shape=jax.ShapeDtypeStruct((normed.shape[0], width), jnp.bfloat16),
        compiler_params=pltpu.CompilerParams(vmem_limit_bytes=16 * 2**20),
        cost_estimate=BRIEF,
        name="project",
    )(y, normed, beside, *pieces)


def partial_kernel(where_ref, own_ref, after_ref, dq_ref, *refs):
    *pieces, out_ref = refs
    core, y = where_ref[1], where_ref[2]
    rows = pl.ds(pl.multiple_of(where_ref[0] * TOK, TOK), TOK)
    grad_kv = (own_ref[rows, :] + after_ref[rows, :].astype(jnp.float32)).astype(jnp.bfloat16)
    for first, piece in zip(piece_columns(y, pieces), pieces):
        count = piece.shape[0]
        grad = lax.dot_general(
            grad_kv, piece[...], (((1,), (1,)), ((), ())), preferred_element_type=jnp.float32
        )
        dq = dq_ref[rows, pl.ds(pl.multiple_of(first % HALF, count), count)]
        grad += jnp.where(first // HALF == core, dq, 0.0)
        out_ref[:, pl.ds(pl.multiple_of(first, count), count)] = grad.astype(out_ref.dtype)


def partial_grad(where, own, after, dq, pieces, kind):
    return pl.pallas_call(
        partial_kernel,
        in_specs=[SCALARS] + [WHOLE] * (3 + len(pieces)),
        out_specs=WHOLE,
        out_shape=jax.ShapeDtypeStruct((TOK, CORES * HALF), kind),
        compiler_params=pltpu.CompilerParams(vmem_limit_bytes=20 * 2**20),
        cost_estimate=BRIEF,
        name="partial_grad",
    )(where, own, after, dq, *pieces)


def input_grad_kernel(
    own_ref, other_ref, x_ref, upper_ref, gain_ref, up_ref, down_ref, gain_grad_ref, grad_ref
):
    features = x_ref.shape[1]
    width = 512
    blocks = [slice(at, at + width) for at in range(0, features, width)]
    squares = jnp.zeros((TOK, 1), jnp.float32)
    for cols in blocks:
        part = x_ref[:, cols].astype(jnp.float32)
        squares += jnp.sum(part * part, axis=-1, keepdims=True)
    inv_rms = lax.rsqrt(squares / features + EPSILON)
    inner = jnp.zeros((TOK, 1), jnp.float32)
    for cols in blocks:
        grad = own_ref[:, cols] + other_ref[:, cols].astype(jnp.float32)
        scaled = x_ref[:, cols].astype(jnp.float32) * inv_rms
        product = grad * scaled
        gain_grad_ref[:, cols] = jnp.sum(product, axis=0, keepdims=True)
        gain = gain_ref[:, cols]
        inner += jnp.sum(product * gain, axis=-1, keepdims=True)
        grad_ref[:, cols] = grad * gain
    mean = inner * (1.0 / features)
    for first, ref in ((0, up_ref), (TOK // 2, down_ref)):
        rows = slice(first, first + TOK // 2)
        for cols in blocks:
            scaled = x_ref[rows, cols].astype(jnp.float32) * inv_rms[rows]
            out = inv_rms[rows] * (grad_ref[rows, cols] - scaled * mean[rows])
            ref[:, cols] = (out + upper_ref[rows, cols].astype(jnp.float32)).astype(jnp.bfloat16)


def input_grad(own, other, x, upper, gain_row):
    features = x.shape[1]
    return pl.pallas_call(
        input_grad_kernel,
        in_specs=[WHOLE] * 5,
        out_specs=[WHOLE] * 3,
        out_shape=[
            jax.ShapeDtypeStruct((TOK // 2, features), jnp.bfloat16),
            jax.ShapeDtypeStruct((TOK // 2, features), jnp.bfloat16),
            jax.ShapeDtypeStruct((1, features), jnp.float32),
        ],
        scratch_shapes=[pltpu.VMEM((TOK, features), jnp.float32)],
        compiler_params=pltpu.CompilerParams(vmem_limit_bytes=16 * 2**20),
        cost_estimate=BRIEF,
        name="input_grad",
    )(own, other, x, upper, gain_row)


def in_three(value):
    terms = []
    for _ in range(3):
        term = lax.reduce_precision(value, 8, 7)
        terms.append(term.astype(jnp.bfloat16))
        value = value - term
    blank = jnp.zeros((value.shape[0], HD - len(terms)), jnp.bfloat16)
    return jnp.concatenate(terms + [blank], axis=1)


def body(section_in, back_in, upstream, gains, kv_weight):
    index = lax.axis_index("ctx").astype(jnp.int32)
    core, z_lo, y = index % CORES, (index // CORES) % Z_LO, index // (CORES * Z_LO)
    place, y_place = index.reshape(1), y.reshape(1)
    x_back, upper_in = back_in[0], upstream[0]

    chip_x_fwd = chip_rows(section_in[0], swap(section_in[0]), core)
    crossing = columns_of(chip_x_fwd, core)
    gain_here = direct(columns_of(gains, core), 1)
    run, gain_here = gather_run(kv_weight[0], core, z_lo, gain_here)
    later_x, later_upper, run, crossing = lax.optimization_barrier((x_back, upper_in, run, crossing))
    chip_x_back = chip_rows(x_back, swap(later_x), core)
    chip_back, _ = norm_forward(chip_x_back, gains)
    chip_fwd, inv_fwd = norm_forward(chip_x_fwd, gains)
    chip_upper = chip_columns(later_upper, core)

    pieces, crossed = gather_weight(run, crossing)
    chip_back, chip_fwd, chip_upper, norms = lax.optimization_barrier(
        (chip_back, chip_fwd, chip_upper, in_three(inv_fwd))
    )

    kv_back = project(y_place, chip_back, pieces, norms, False)
    before = to_next_chip(kv_back)
    kv_here = direct(project(y_place, chip_fwd, pieces, norms, True), 1)

    dq, grad_before, grad_own = backward_attention(place, chip_back, chip_upper, before, kv_back)
    after, kv_here, crossed = lax.optimization_barrier(
        (to_chip_before(grad_before), kv_here, crossed)
    )

    def partial(row, kind):
        return partial_grad(jnp.stack([row, core, y]), grad_own, after, dq, pieces, kind)

    away = swap(partial(1 - core, jnp.bfloat16))
    home = partial(core, jnp.float32)
    up, down, gain_grad = input_grad(home, away, x_back, upper_in, gains)
    up_half, down_half = halfway(up, UP), halfway(down, DOWN)

    kv_here, _ = lax.optimization_barrier((kv_here, up))
    before_here = to_next_chip(kv_here)
    gain_grad = gain_grad + swap(gain_grad)
    for bit in (1, 2, 4):
        gain_grad = gain_grad + over_ctx(gain_grad, lambda y, z, c: (y ^ bit, z, c))
    up_half, down_half, gain_grad, crossed = lax.optimization_barrier(
        (up_half, down_half, gain_grad, crossed)
    )
    up, down = arrive(up_half, UP, -1), arrive(down_half, DOWN, -1)
    gain_grad = gain_grad + over_ctx(gain_grad, lambda y, z, c: (y, z ^ 1, c))
    up, down, gain_grad = lax.optimization_barrier((up, down, gain_grad))
    gain_grad = gain_grad + over_ctx(gain_grad, lambda y, z, c: (y, z ^ 2, c))
    next_grad = jnp.concatenate([up, down], axis=0)

    out = forward_attention(place, crossed, gain_here, before_here, kv_here)
    first, second = out[:TOK], out[TOK:]
    mine = jnp.where(core == 0, first, second)
    other = swap(jnp.where(core == 0, second, first))
    next_in = jnp.concatenate(
        [jnp.where(core == 0, mine, other), jnp.where(core == 0, other, mine)], axis=1
    )
    return (next_in[None], next_grad[None], gain_grad)


def solution(mesh):
    in_specs = (
        P("section", "ctx", None),
        P("section", "ctx", None),
        P("section", "ctx", None),
        P("section", None),
        P("section", "ctx", None),
    )
    out_specs = (P("section", "ctx", None), P("section", "ctx", None), P("section", None))
    return jax.shard_map(body, mesh=mesh, in_specs=in_specs, out_specs=out_specs, check_vma=False)
```

```python
import functools

import jax
import jax.numpy as jnp
from jax import lax
from jax.experimental import pallas as pl
from jax.experimental.pallas import tpu as pltpu
from jax.sharding import PartitionSpec as P

HD = 128
STEPS = 2
EPSILON = 1e-05
GROUP = 8
KVH = 4
TOK = 128
SPAN = (STEPS + 1) * TOK

X, Z_HI, Y, Z_LO, CORES = 4, 2, 8, 4, 2
Z = Z_HI * Z_LO
CHIPS = Y * Z_LO
CTX = Y * Z_LO * CORES

HEADS = KVH // CORES
CHIP_TOK = CORES * TOK
HALF = HEADS * GROUP * HD

SCALE = HD ** (-0.5)
LOG2E = 1.4426950408889634


def ctx_pairs(move):
    pairs = []
    for c in range(CTX):
        target = move(c // (Z_LO * CORES), (c // CORES) % Z_LO, c % CORES)
        if target is not None:
            y, z_lo, core = target
            pairs.append((c, (y * Z_LO + z_lo) * CORES + core))
    return pairs


def over_ctx(value, move):
    return lax.ppermute(value, "ctx", ctx_pairs(move))


def grid_pairs(move):
    pairs = []
    for x in range(X):
        for z in range(Z):
            for core in range(CORES):
                new_x, new_z = move(x, z, core)
                new_x, new_z = (new_x % X, new_z % Z)
                for y in range(Y):
                    source = (x * Z_HI + z // Z_LO) * CTX + (y * Z_LO + z % Z_LO) * CORES + core
                    target = (new_x * Z_HI + new_z // Z_LO) * CTX + (y * Z_LO + new_z % Z_LO) * CORES + core
                    pairs.append((source, target))
    return pairs


def over_grid(value, move):
    return lax.ppermute(value, ("section", "ctx"), grid_pairs(move))


WAY = (2, -2)


def halfway(value):
    return over_grid(value, lambda x, z, core: (x, z + WAY[core]))


def arrive(value, distance):
    def move(x, z, core):
        z_hi = ((z - WAY[core]) % Z) // Z_LO
        cross = (1 if z_hi == Z_HI - 1 else 0) if distance == 1 else (-1 if z_hi == 0 else 0)
        return (x + cross, z + WAY[core])

    return over_grid(value, move)


def norm_forward(section_x, gain_row):
    values = section_x.astype(jnp.float32)
    inv_rms = lax.rsqrt(jnp.mean(values * values, axis=-1, keepdims=True) + EPSILON)
    return (values * inv_rms * gain_row).astype(jnp.bfloat16), inv_rms


def by_head(kv_columns):
    parts = []
    for head in range(KVH):
        parts.append(kv_columns[:, head * HD : (head + 1) * HD])
        parts.append(kv_columns[:, (KVH + head) * HD : (KVH + head + 1) * HD])
    return jnp.concatenate(parts, axis=1)


def gather_run(own_rows, core, z_lo):
    half = own_rows.shape[1] // 2
    columns = by_head(own_rows)
    low, high = columns[:, :half], columns[:, half:]
    keep = jnp.where(core == 0, low, high)
    received = swap(jnp.where(core == 0, high, low))
    chip = chip_rows(keep, received, core)
    rows = chip.shape[0]
    pieces = [chip]
    for step in range(1, Z_LO):
        pieces.append(over_ctx(chip, lambda y, z, c, step=step: (y, (z + step) % Z_LO, c)))
    back = pieces[::-1]
    return lax.dynamic_slice_in_dim(
        jnp.concatenate(back + back[:-1], axis=0), (Z_LO - 1 - z_lo) * rows, Z_LO * rows, 0
    )


def gather_weight(run, crossing):
    def up(piece):
        return over_ctx(piece, lambda y, z, c: ((y + 1) % Y, z, c))

    def down(piece):
        return over_ctx(piece, lambda y, z, c: ((y - 1) % Y, z, c))

    crossing = halfway(crossing)
    rising, falling = [up(run)], [down(run)]
    rising.append(up(rising[0]))
    falling.append(down(falling[0]))
    rising[1], falling[1], crossing = lax.optimization_barrier((rising[1], falling[1], crossing))
    rising.append(up(rising[1]))
    falling.append(down(falling[1]))
    middle = run.shape[0] // 2
    rising.append(up(rising[2][:middle]))
    falling.append(down(falling[2][middle:]))
    pieces = [run, *falling[:3], rising[3], falling[3], *rising[:3][::-1]]
    return pieces, arrive(crossing, 1), rising[0]


def swap(value):
    return over_ctx(value, lambda y, z, c: (y, z, 1 - c))


def chip_rows(own, partner, core):
    return jnp.concatenate(
        [jnp.where(core == 0, own, partner), jnp.where(core == 0, partner, own)], axis=0
    )


def to_next_chip(value):
    pairs = [(i, i + CORES) for i in range(CTX - CORES)]
    return lax.ppermute(value, "ctx", pairs)


def to_chip_before(value):
    pairs = [(i, i - CORES) for i in range(CORES, CTX)]
    return lax.ppermute(value, "ctx", pairs)


def columns_of(value, core):
    return lax.dynamic_slice_in_dim(value, core * HALF, HALF, 1)


def chip_columns(value, core):
    return chip_rows(columns_of(value, core), swap(columns_of(value, 1 - core)), core)


def stacked(ref, tokens):
    rows = slice(tokens * TOK, (tokens + 1) * TOK)
    return jnp.concatenate([ref[rows, g * HD : (g + 1) * HD] for g in range(GROUP)], axis=0)


def masked_scores(keys, queries, tokens, any_before):
    scores = lax.dot_general(
        keys, queries, (((1,), (1,)), ((), ())), preferred_element_type=jnp.float32
    )
    across = queries.shape[0]
    before = (STEPS - tokens) * TOK
    seen = lax.broadcasted_iota(jnp.int32, (TOK, across), 0)
    query = lax.broadcasted_iota(jnp.int32, (TOK, across), 1) % TOK
    parts = [jnp.where(any_before, scores[:before], -1e30)]
    if tokens:
        parts.append(scores[before : STEPS * TOK])
    parts.append(jnp.where(seen <= query, scores[STEPS * TOK :], -1e30))
    return jnp.concatenate(parts, axis=0)


PAIR = 2
WIDE = GROUP * HD

BESIDE = HALF // (2 * HEADS * HD) + 1

BRIEF = pl.CostEstimate(flops=1000, bytes_accessed=1000, transcendentals=0)


def forward_kernel(index_ref, x_ref, beside_ref, before_ref, own_ref, out_ref):
    any_before = index_ref[0] >= CORES
    beside = beside_ref[...].astype(jnp.float32)
    beside = beside[:BESIDE] + beside[BESIDE : 2 * BESIDE] + beside[2 * BESIDE : 3 * BESIDE]
    per_head = WIDE // beside.shape[1]
    head = pl.program_id(0)
    gain_rows = jnp.where(head == 0, beside[:per_head], beside[per_head : 2 * per_head])
    gain = jnp.concatenate([gain_rows[i : i + 1] for i in range(per_head)], axis=1)
    inv_row = beside[2 * per_head : 2 * per_head + 1, :CHIP_TOK]
    inv_rms = jnp.broadcast_to(inv_row, (HD, CHIP_TOK)).T
    keys = jnp.concatenate([before_ref[:, :HD], own_ref[:, :HD]], axis=0)
    values = jnp.concatenate([before_ref[:, HD:], own_ref[:, HD:]], axis=0)
    values_t = values.astype(jnp.float32).T.astype(jnp.bfloat16)
    for tokens in range(CORES):
        span = slice(tokens * TOK, tokens * TOK + SPAN)
        rows = slice(tokens * TOK, (tokens + 1) * TOK)
        inv = inv_rms[rows]
        for pair in range(GROUP // PAIR):
            cols = [
                slice(g * HD, (g + 1) * HD) for g in range(pair * PAIR, (pair + 1) * PAIR)
            ]
            x = [x_ref[rows, at].astype(jnp.float32) for at in cols]
            queries = jnp.concatenate(
                [(part * inv * gain[:, at]).astype(jnp.bfloat16) for part, at in zip(x, cols)],
                axis=0,
            )
            scores = masked_scores(keys[span], queries, tokens, any_before)
            top = jnp.max(scores, axis=0, keepdims=True)
            terms = jnp.exp2((scores - top) * (SCALE * LOG2E))
            total = jnp.sum(terms, axis=0, keepdims=True)
            attended = jnp.dot(
                values_t[:, span], terms.astype(jnp.bfloat16), preferred_element_type=jnp.float32
            ) * (1.0 / total)
            for g, at in enumerate(cols):
                out = attended[:, g * TOK : (g + 1) * TOK].T + x[g]
                out_ref[rows, at] = out.astype(jnp.bfloat16)


def forward_attention(index, crossed, before, own):
    heads = pl.BlockSpec((CHIP_TOK, WIDE), lambda h, index: (0, h))
    kv = pl.BlockSpec((CHIP_TOK, 2 * HD), lambda h, index: (0, h))
    return pl.pallas_call(
        forward_kernel,
        grid_spec=pltpu.PrefetchScalarGridSpec(
            num_scalar_prefetch=1,
            grid=(HEADS,),
            in_specs=[
                heads,
                pl.BlockSpec((16, own.shape[1]), lambda h, index: (CHIP_TOK // 16, 0)),
                kv,
                kv,
            ],
            out_specs=heads,
        ),
        out_shape=jax.ShapeDtypeStruct((CHIP_TOK, HALF), jnp.bfloat16),
        compiler_params=pltpu.CompilerParams(vmem_limit_bytes=20 * 2**20),
        cost_estimate=BRIEF,
        name="forward_attention",
    )(index, crossed, own, before, own)


def backward_kernel(
    index_ref, normed_ref, upper_ref, before_ref, own_ref, dq_ref, grad_before_ref, grad_own_ref,
    probs_ref, dlog_ref,
):
    any_before = index_ref[0] >= CORES
    keys = jnp.concatenate([before_ref[:, :HD], own_ref[:, :HD]], axis=0)
    values = jnp.concatenate([before_ref[:, HD:], own_ref[:, HD:]], axis=0)
    keys_t = keys.astype(jnp.float32).T.astype(jnp.bfloat16)
    queries = [stacked(normed_ref, tokens) for tokens in range(CORES)]
    uppers = [stacked(upper_ref, tokens) for tokens in range(CORES)]
    for tokens in range(CORES):
        span = slice(tokens * TOK, tokens * TOK + SPAN)
        for pair in range(GROUP // PAIR):
            these = slice(pair * PAIR * TOK, (pair + 1) * PAIR * TOK)
            scores = masked_scores(keys[span], queries[tokens][these], tokens, any_before)
            grad_probs = lax.dot_general(
                values[span],
                uppers[tokens][these],
                (((1,), (1,)), ((), ())),
                preferred_element_type=jnp.float32,
            )
            top = jnp.max(scores, axis=0, keepdims=True)
            terms = jnp.exp2((scores - top) * (SCALE * LOG2E))
            inverse = 1.0 / jnp.sum(terms, axis=0, keepdims=True)
            row_dot = jnp.sum(terms * grad_probs, axis=0, keepdims=True) * inverse
            probs = terms * inverse
            cols = slice(tokens * WIDE + these.start, tokens * WIDE + these.stop)
            probs_ref[span, cols] = probs.astype(jnp.bfloat16)
            dlog_ref[span, cols] = (probs * ((grad_probs - row_dot) * SCALE)).astype(jnp.bfloat16)
        dlogits = dlog_ref[span, tokens * WIDE : (tokens + 1) * WIDE]
        grad_query = jnp.dot(keys_t[:, span], dlogits, preferred_element_type=jnp.float32)
        rows = slice(tokens * TOK, (tokens + 1) * TOK)
        for g in range(GROUP):
            dq_ref[rows, g * HD : (g + 1) * HD] = grad_query[:, g * TOK : (g + 1) * TOK].T
    for left, factors, first in ((dlog_ref, queries, 0), (probs_ref, uppers, HD)):
        cols = slice(first, first + HD)

        def product(rows, tokens, last):
            factor = jnp.concatenate(factors[tokens:last], axis=0)
            return jnp.dot(
                left[rows, tokens * WIDE : last * WIDE], factor, preferred_element_type=jnp.float32
            )

        middle = product(slice(TOK, 3 * TOK), 0, 2)
        grad_before_ref[:TOK, cols] = product(slice(0, TOK), 0, 1).astype(jnp.bfloat16)
        grad_before_ref[TOK:, cols] = middle[:TOK].astype(jnp.bfloat16)
        grad_own_ref[:TOK, cols] = middle[TOK:]
        grad_own_ref[TOK:, cols] = product(slice(3 * TOK, 4 * TOK), 1, 2)


def backward_attention(index, normed, upper, before, own):
    kv = pl.BlockSpec((CHIP_TOK, 2 * HD), lambda h, index: (0, h))
    heads = pl.BlockSpec((CHIP_TOK, WIDE), lambda h, index: (0, h))
    return pl.pallas_call(
        backward_kernel,
        grid_spec=pltpu.PrefetchScalarGridSpec(
            num_scalar_prefetch=1,
            grid=(HEADS,),
            in_specs=[
                pl.BlockSpec((CHIP_TOK, WIDE), lambda h, index: (0, (index[0] % CORES) * HEADS + h)),
                heads,
                kv,
                kv,
            ],
            out_specs=[heads, kv, kv],
            scratch_shapes=[
                pltpu.VMEM((4 * TOK, CORES * WIDE), jnp.bfloat16),
                pltpu.VMEM((4 * TOK, CORES * WIDE), jnp.bfloat16),
            ],
        ),
        out_shape=[
            jax.ShapeDtypeStruct((CHIP_TOK, HALF), jnp.float32),
            jax.ShapeDtypeStruct(before.shape, jnp.bfloat16),
            jax.ShapeDtypeStruct(own.shape, jnp.float32),
        ],
        compiler_params=pltpu.CompilerParams(vmem_limit_bytes=24 * 2**20),
        cost_estimate=pl.CostEstimate(flops=3*10**9, bytes_accessed=10**6, transcendentals=0),
        name="backward_attention",
    )(index, normed, upper, before, own)


def piece_columns(y, pieces):
    firsts, at = [], 0
    block = pieces[0].shape[0]
    for piece in pieces:
        firsts.append(pl.multiple_of(((y + at // block) % Y) * block, block) + at % block)
        at += piece.shape[0]
    return firsts


def project_kernel(y_ref, normed_ref, beside_ref, *refs):
    *pieces, out_ref = refs
    width = pieces[0].shape[1]
    total = jnp.zeros((normed_ref.shape[0], width), jnp.float32)
    for first, piece in zip(piece_columns(y_ref[0], pieces), pieces):
        rows = piece.shape[0]
        part = normed_ref[:, pl.ds(pl.multiple_of(first, rows), rows)]
        total += jnp.dot(part, piece[...], preferred_element_type=jnp.float32)
    rows = total.shape[0]
    out_ref[:rows, :] = total.astype(out_ref.dtype)
    if out_ref.shape[0] > rows:
        out_ref[rows:, :] = beside_ref[...]


SCALARS = pl.BlockSpec(memory_space=pltpu.SMEM)
WHOLE = pl.BlockSpec(memory_space=pltpu.VMEM)


def project(y, normed, pieces, beside, with_beside):
    rows = normed.shape[0] + (beside.shape[0] if with_beside else 0)
    return pl.pallas_call(
        project_kernel,
        in_specs=[SCALARS] + [WHOLE] * (2 + len(pieces)),
        out_specs=WHOLE,
        out_shape=jax.ShapeDtypeStruct((rows, pieces[0].shape[1]), jnp.bfloat16),
        compiler_params=pltpu.CompilerParams(vmem_limit_bytes=16 * 2**20),
        cost_estimate=BRIEF,
        name="project",
    )(y, normed, beside, *pieces)


def partial_kernel(where_ref, own_ref, after_ref, dq_ref, *refs):
    *pieces, out_ref = refs
    core, y = where_ref[1], where_ref[2]
    rows = pl.ds(pl.multiple_of(where_ref[0] * TOK, TOK), TOK)
    grad_kv = (own_ref[rows, :] + after_ref[rows, :].astype(jnp.float32)).astype(jnp.bfloat16)
    for first, piece in zip(piece_columns(y, pieces), pieces):
        count = piece.shape[0]
        grad = lax.dot_general(
            grad_kv, piece[...], (((1,), (1,)), ((), ())), preferred_element_type=jnp.float32
        )
        dq = dq_ref[rows, pl.ds(pl.multiple_of(first % HALF, count), count)]
        grad += jnp.where(first // HALF == core, dq, 0.0)
        out_ref[:, pl.ds(pl.multiple_of(first, count), count)] = grad.astype(out_ref.dtype)


def partial_grad(where, own, after, dq, pieces, kind):
    return pl.pallas_call(
        partial_kernel,
        in_specs=[SCALARS] + [WHOLE] * (3 + len(pieces)),
        out_specs=WHOLE,
        out_shape=jax.ShapeDtypeStruct((TOK, CORES * HALF), kind),
        compiler_params=pltpu.CompilerParams(vmem_limit_bytes=20 * 2**20),
        cost_estimate=BRIEF,
        name="partial_grad",
    )(where, own, after, dq, *pieces)


def input_grad_kernel(
    own_ref, other_ref, x_ref, upper_ref, gain_ref, out_ref, gain_grad_ref, grad_ref
):
    features = x_ref.shape[1]
    width = 512
    blocks = [slice(at, at + width) for at in range(0, features, width)]
    squares = jnp.zeros((TOK, 1), jnp.float32)
    for cols in blocks:
        part = x_ref[:, cols].astype(jnp.float32)
        squares += jnp.sum(part * part, axis=-1, keepdims=True)
    inv_rms = lax.rsqrt(squares / features + EPSILON)
    inner = jnp.zeros((TOK, 1), jnp.float32)
    for cols in blocks:
        grad = own_ref[:, cols] + other_ref[:, cols].astype(jnp.float32)
        scaled = x_ref[:, cols].astype(jnp.float32) * inv_rms
        product = grad * scaled
        gain_grad_ref[:, cols] = jnp.sum(product, axis=0, keepdims=True)
        gain = gain_ref[:, cols]
        inner += jnp.sum(product * gain, axis=-1, keepdims=True)
        grad_ref[:, cols] = grad * gain
    mean = inner * (1.0 / features)
    for cols in blocks:
        scaled = x_ref[:, cols].astype(jnp.float32) * inv_rms
        out = inv_rms * (grad_ref[:, cols] - scaled * mean)
        out_ref[:, cols] = (out + upper_ref[:, cols].astype(jnp.float32)).astype(jnp.bfloat16)


def input_grad(own, other, x, upper, gain_row):
    features = x.shape[1]
    return pl.pallas_call(
        input_grad_kernel,
        in_specs=[WHOLE] * 5,
        out_specs=[WHOLE] * 2,
        out_shape=[
            jax.ShapeDtypeStruct((TOK, features), jnp.bfloat16),
            jax.ShapeDtypeStruct((1, features), jnp.float32),
        ],
        scratch_shapes=[pltpu.VMEM((TOK, features), jnp.float32)],
        compiler_params=pltpu.CompilerParams(vmem_limit_bytes=16 * 2**20),
        cost_estimate=BRIEF,
        name="input_grad",
    )(own, other, x, upper, gain_row)


def in_three(value):
    terms = []
    for _ in range(3):
        term = lax.reduce_precision(value, 8, 7)
        terms.append(term.astype(jnp.bfloat16))
        value = value - term
    return jnp.concatenate(terms, axis=0)


def body(section_in, back_in, upstream, gains, kv_weight):
    index = lax.axis_index("ctx").astype(jnp.int32)
    core, z_lo, y = index % CORES, (index // CORES) % Z_LO, index // (CORES * Z_LO)
    place, y_place = index.reshape(1), y.reshape(1)
    x_back, upper_in = back_in[0], upstream[0]

    chip_x_fwd = chip_rows(section_in[0], swap(section_in[0]), core)
    crossing = columns_of(chip_x_fwd, core)
    run, crossing = lax.optimization_barrier((gather_run(kv_weight[0], core, z_lo), crossing))
    pieces, crossed, first_step = gather_weight(run, crossing)

    later_x, later_upper, _ = lax.optimization_barrier((x_back, upper_in, first_step))
    chip_x_back = chip_rows(x_back, swap(later_x), core)
    chip_back, _ = norm_forward(chip_x_back, gains)
    chip_fwd, inv_fwd = norm_forward(chip_x_fwd, gains)
    chip_upper = chip_columns(later_upper, core)

    width = pieces[0].shape[1]
    norms = jnp.pad(inv_fwd.reshape(1, CHIP_TOK), ((0, 0), (0, width - CHIP_TOK)))
    beside = in_three(jnp.concatenate([columns_of(gains, core).reshape(-1, width), norms], axis=0))
    beside = jnp.pad(beside, ((0, 16 - beside.shape[0]), (0, 0)))
    chip_back, chip_fwd, chip_upper, beside = lax.optimization_barrier(
        (chip_back, chip_fwd, chip_upper, beside)
    )

    kv_back = project(y_place, chip_back, pieces, beside, False)
    kv_back, chip_fwd = lax.optimization_barrier((kv_back, chip_fwd))
    before = to_next_chip(kv_back)
    kv_half = halfway(project(y_place, chip_fwd, pieces, beside, True))

    dq, grad_before, grad_own = backward_attention(place, chip_back, chip_upper, before, kv_back)
    kv_half, grad_before = lax.optimization_barrier((kv_half, grad_before))
    after, kv_here, crossed = lax.optimization_barrier(
        (to_chip_before(grad_before), arrive(kv_half, 1), crossed)
    )

    def partial(row, kind):
        return partial_grad(jnp.stack([row, core, y]), grad_own, after, dq, pieces, kind)

    away = swap(partial(1 - core, jnp.bfloat16))
    home = partial(core, jnp.float32)
    grad_in, gain_grad = input_grad(home, away, x_back, upper_in, gains)
    half_sent = halfway(grad_in)

    kv_here, _ = lax.optimization_barrier((kv_here, grad_in))
    before_here = to_next_chip(kv_here)
    gain_grad = gain_grad + swap(gain_grad)
    for bit in (1, 2, 4):
        gain_grad = gain_grad + over_ctx(gain_grad, lambda y, z, c: (y ^ bit, z, c))
    half_sent, gain_grad, crossed = lax.optimization_barrier((half_sent, gain_grad, crossed))
    next_grad = arrive(half_sent, -1)
    gain_grad = gain_grad + over_ctx(gain_grad, lambda y, z, c: (y, z ^ 1, c))
    next_grad, gain_grad = lax.optimization_barrier((next_grad, gain_grad))
    gain_grad = gain_grad + over_ctx(gain_grad, lambda y, z, c: (y, z ^ 2, c))

    out = forward_attention(place, crossed, before_here, kv_here)
    first, second = out[:TOK], out[TOK:]
    mine = jnp.where(core == 0, first, second)
    other = swap(jnp.where(core == 0, second, first))
    next_in = jnp.concatenate(
        [jnp.where(core == 0, mine, other), jnp.where(core == 0, other, mine)], axis=1
    )
    return (next_in[None], next_grad[None], gain_grad)


def solution(mesh):
    in_specs = (
        P("section", "ctx", None),
        P("section", "ctx", None),
        P("section", "ctx", None),
        P("section", None),
        P("section", "ctx", None),
    )
    out_specs = (P("section", "ctx", None), P("section", "ctx", None), P("section", None))
    return jax.shard_map(body, mesh=mesh, in_specs=in_specs, out_specs=out_specs, check_vma=False)
```

```python
import functools

import jax
import jax.numpy as jnp
from jax import lax
from jax.experimental import pallas as pl
from jax.experimental.pallas import tpu as pltpu
from jax.sharding import PartitionSpec as P

HD = 128
STEPS = 2
EPSILON = 1e-05
GROUP = 8
KVH = 4
TOK = 128
SPAN = (STEPS + 1) * TOK

X, Z_HI, Y, Z_LO, CORES = 4, 2, 8, 4, 2
Z = Z_HI * Z_LO
CHIPS = Y * Z_LO
CTX = Y * Z_LO * CORES

HEADS = KVH // CORES
CHIP_TOK = CORES * TOK
HALF = HEADS * GROUP * HD

SCALE = HD ** (-0.5)
LOG2E = 1.4426950408889634


def ctx_pairs(move):
    pairs = []
    for c in range(CTX):
        target = move(c // (Z_LO * CORES), (c // CORES) % Z_LO, c % CORES)
        if target is not None:
            y, z_lo, core = target
            pairs.append((c, (y * Z_LO + z_lo) * CORES + core))
    return pairs


def over_ctx(value, move):
    return lax.ppermute(value, "ctx", ctx_pairs(move))


def grid_pairs(move):
    pairs = []
    for x in range(X):
        for z in range(Z):
            for core in range(CORES):
                new_x, new_z = move(x, z, core)
                new_x, new_z = (new_x % X, new_z % Z)
                for y in range(Y):
                    source = (x * Z_HI + z // Z_LO) * CTX + (y * Z_LO + z % Z_LO) * CORES + core
                    target = (new_x * Z_HI + new_z // Z_LO) * CTX + (y * Z_LO + new_z % Z_LO) * CORES + core
                    pairs.append((source, target))
    return pairs


def over_grid(value, move):
    return lax.ppermute(value, ("section", "ctx"), grid_pairs(move))


WAY = (2, -2)


def halfway(value):
    return over_grid(value, lambda x, z, core: (x, z + WAY[core]))


def arrive(value, distance):
    def move(x, z, core):
        z_hi = ((z - WAY[core]) % Z) // Z_LO
        cross = (1 if z_hi == Z_HI - 1 else 0) if distance == 1 else (-1 if z_hi == 0 else 0)
        return (x + cross, z + WAY[core])

    return over_grid(value, move)


def norm_forward(section_x, gain_row):
    values = section_x.astype(jnp.float32)
    inv_rms = lax.rsqrt(jnp.mean(values * values, axis=-1, keepdims=True) + EPSILON)
    return (values * inv_rms * gain_row).astype(jnp.bfloat16), inv_rms


def by_head(kv_columns):
    parts = []
    for head in range(KVH):
        parts.append(kv_columns[:, head * HD : (head + 1) * HD])
        parts.append(kv_columns[:, (KVH + head) * HD : (KVH + head + 1) * HD])
    return jnp.concatenate(parts, axis=1)


def gather_run(own_rows, core, z_lo):
    half = own_rows.shape[1] // 2
    columns = by_head(own_rows)
    low, high = columns[:, :half], columns[:, half:]
    keep = jnp.where(core == 0, low, high)
    received = swap(jnp.where(core == 0, high, low))
    chip = chip_rows(keep, received, core)
    rows = chip.shape[0]
    pieces = [chip]
    for step in range(1, Z_LO):
        pieces.append(over_ctx(chip, lambda y, z, c, step=step: (y, (z + step) % Z_LO, c)))
    back = pieces[::-1]
    return lax.dynamic_slice_in_dim(
        jnp.concatenate(back + back[:-1], axis=0), (Z_LO - 1 - z_lo) * rows, Z_LO * rows, 0
    )


def gather_weight(run, crossing):
    def up(piece):
        return over_ctx(piece, lambda y, z, c: ((y + 1) % Y, z, c))

    def down(piece):
        return over_ctx(piece, lambda y, z, c: ((y - 1) % Y, z, c))

    crossing = halfway(crossing)
    rising, falling = [up(run)], [down(run)]
    rising.append(up(rising[0]))
    falling.append(down(falling[0]))
    rising[1], falling[1], crossing = lax.optimization_barrier((rising[1], falling[1], crossing))
    rising.append(up(rising[1]))
    falling.append(down(falling[1]))
    middle = run.shape[0] // 2
    rising.append(up(rising[2][:middle]))
    falling.append(down(falling[2][middle:]))
    pieces = [run, *falling[:3], rising[3], falling[3], *rising[:3][::-1]]
    return pieces, arrive(crossing, 1), falling[0]


def swap(value):
    return over_ctx(value, lambda y, z, c: (y, z, 1 - c))


def chip_rows(own, partner, core):
    return jnp.concatenate(
        [jnp.where(core == 0, own, partner), jnp.where(core == 0, partner, own)], axis=0
    )


def to_next_chip(value):
    pairs = [(i, i + CORES) for i in range(CTX - CORES)]
    return lax.ppermute(value, "ctx", pairs)


def to_chip_before(value):
    pairs = [(i, i - CORES) for i in range(CORES, CTX)]
    return lax.ppermute(value, "ctx", pairs)


def columns_of(value, core):
    return lax.dynamic_slice_in_dim(value, core * HALF, HALF, 1)


def chip_columns(value, core):
    return chip_rows(columns_of(value, core), swap(columns_of(value, 1 - core)), core)


def stacked(ref, tokens):
    rows = slice(tokens * TOK, (tokens + 1) * TOK)
    return jnp.concatenate([ref[rows, g * HD : (g + 1) * HD] for g in range(GROUP)], axis=0)


def masked_scores(keys, queries, tokens, any_before):
    scores = lax.dot_general(
        keys, queries, (((1,), (1,)), ((), ())), preferred_element_type=jnp.float32
    )
    across = queries.shape[0]
    before = (STEPS - tokens) * TOK
    seen = lax.broadcasted_iota(jnp.int32, (TOK, across), 0)
    query = lax.broadcasted_iota(jnp.int32, (TOK, across), 1) % TOK
    parts = [jnp.where(any_before, scores[:before], -1e30)]
    if tokens:
        parts.append(scores[before : STEPS * TOK])
    parts.append(jnp.where(seen <= query, scores[STEPS * TOK :], -1e30))
    return jnp.concatenate(parts, axis=0)


PAIR = 2
WIDE = GROUP * HD

BESIDE = HALF // (2 * HEADS * HD) + 1

BRIEF = pl.CostEstimate(flops=1000, bytes_accessed=1000, transcendentals=0)


def forward_kernel(index_ref, x_ref, beside_ref, before_ref, own_ref, out_ref):
    any_before = index_ref[0] >= CORES
    beside = beside_ref[...].astype(jnp.float32)
    beside = beside[:BESIDE] + beside[BESIDE : 2 * BESIDE] + beside[2 * BESIDE : 3 * BESIDE]
    per_head = WIDE // beside.shape[1]
    head = pl.program_id(0)
    gain_rows = jnp.where(head == 0, beside[:per_head], beside[per_head : 2 * per_head])
    gain = jnp.concatenate([gain_rows[i : i + 1] for i in range(per_head)], axis=1)
    inv_row = beside[2 * per_head : 2 * per_head + 1, :CHIP_TOK]
    inv_rms = jnp.broadcast_to(inv_row, (HD, CHIP_TOK)).T
    keys = jnp.concatenate([before_ref[:, :HD], own_ref[:, :HD]], axis=0)
    values = jnp.concatenate([before_ref[:, HD:], own_ref[:, HD:]], axis=0)
    values_t = values.astype(jnp.float32).T.astype(jnp.bfloat16)
    for tokens in range(CORES):
        span = slice(tokens * TOK, tokens * TOK + SPAN)
        rows = slice(tokens * TOK, (tokens + 1) * TOK)
        inv = inv_rms[rows]
        for pair in range(GROUP // PAIR):
            cols = [
                slice(g * HD, (g + 1) * HD) for g in range(pair * PAIR, (pair + 1) * PAIR)
            ]
            x = [x_ref[rows, at].astype(jnp.float32) for at in cols]
            queries = jnp.concatenate(
                [(part * inv * gain[:, at]).astype(jnp.bfloat16) for part, at in zip(x, cols)],
                axis=0,
            )
            scores = masked_scores(keys[span], queries, tokens, any_before)
            top = jnp.max(scores, axis=0, keepdims=True)
            terms = jnp.exp2((scores - top) * (SCALE * LOG2E))
            total = jnp.sum(terms, axis=0, keepdims=True)
            attended = jnp.dot(
                values_t[:, span], terms.astype(jnp.bfloat16), preferred_element_type=jnp.float32
            ) * (1.0 / total)
            for g, at in enumerate(cols):
                out = attended[:, g * TOK : (g + 1) * TOK].T + x[g]
                out_ref[rows, at] = out.astype(jnp.bfloat16)


def forward_attention(index, crossed, before, own):
    heads = pl.BlockSpec((CHIP_TOK, WIDE), lambda h, index: (0, h))
    kv = pl.BlockSpec((CHIP_TOK, 2 * HD), lambda h, index: (0, h))
    return pl.pallas_call(
        forward_kernel,
        grid_spec=pltpu.PrefetchScalarGridSpec(
            num_scalar_prefetch=1,
            grid=(HEADS,),
            in_specs=[
                heads,
                pl.BlockSpec((16, own.shape[1]), lambda h, index: (CHIP_TOK // 16, 0)),
                kv,
                kv,
            ],
            out_specs=heads,
        ),
        out_shape=jax.ShapeDtypeStruct((CHIP_TOK, HALF), jnp.bfloat16),
        compiler_params=pltpu.CompilerParams(vmem_limit_bytes=20 * 2**20),
        cost_estimate=BRIEF,
        name="forward_attention",
    )(index, crossed, own, before, own)


def backward_kernel(
    index_ref, normed_ref, upper_ref, before_ref, own_ref, dq_ref, grad_before_ref, grad_own_ref,
    probs_ref, dlog_ref,
):
    any_before = index_ref[0] >= CORES
    keys = jnp.concatenate([before_ref[:, :HD], own_ref[:, :HD]], axis=0)
    values = jnp.concatenate([before_ref[:, HD:], own_ref[:, HD:]], axis=0)
    keys_t = keys.astype(jnp.float32).T.astype(jnp.bfloat16)
    queries = [stacked(normed_ref, tokens) for tokens in range(CORES)]
    uppers = [stacked(upper_ref, tokens) for tokens in range(CORES)]
    for tokens in range(CORES):
        span = slice(tokens * TOK, tokens * TOK + SPAN)
        for pair in range(GROUP // PAIR):
            these = slice(pair * PAIR * TOK, (pair + 1) * PAIR * TOK)
            scores = masked_scores(keys[span], queries[tokens][these], tokens, any_before)
            grad_probs = lax.dot_general(
                values[span],
                uppers[tokens][these],
                (((1,), (1,)), ((), ())),
                preferred_element_type=jnp.float32,
            )
            top = jnp.max(scores, axis=0, keepdims=True)
            terms = jnp.exp2((scores - top) * (SCALE * LOG2E))
            inverse = 1.0 / jnp.sum(terms, axis=0, keepdims=True)
            row_dot = jnp.sum(terms * grad_probs, axis=0, keepdims=True) * inverse
            probs = terms * inverse
            cols = slice(tokens * WIDE + these.start, tokens * WIDE + these.stop)
            probs_ref[span, cols] = probs.astype(jnp.bfloat16)
            dlog_ref[span, cols] = (probs * ((grad_probs - row_dot) * SCALE)).astype(jnp.bfloat16)
        dlogits = dlog_ref[span, tokens * WIDE : (tokens + 1) * WIDE]
        grad_query = jnp.dot(keys_t[:, span], dlogits, preferred_element_type=jnp.float32)
        rows = slice(tokens * TOK, (tokens + 1) * TOK)
        for g in range(GROUP):
            dq_ref[rows, g * HD : (g + 1) * HD] = grad_query[:, g * TOK : (g + 1) * TOK].T
    for left, factors, first in ((dlog_ref, queries, 0), (probs_ref, uppers, HD)):
        cols = slice(first, first + HD)

        def product(rows, tokens, last):
            factor = jnp.concatenate(factors[tokens:last], axis=0)
            return jnp.dot(
                left[rows, tokens * WIDE : last * WIDE], factor, preferred_element_type=jnp.float32
            )

        middle = product(slice(TOK, 3 * TOK), 0, 2)
        grad_before_ref[:TOK, cols] = product(slice(0, TOK), 0, 1).astype(jnp.bfloat16)
        grad_before_ref[TOK:, cols] = middle[:TOK].astype(jnp.bfloat16)
        grad_own_ref[:TOK, cols] = middle[TOK:]
        grad_own_ref[TOK:, cols] = product(slice(3 * TOK, 4 * TOK), 1, 2)


def backward_attention(index, normed, upper, before, own):
    kv = pl.BlockSpec((CHIP_TOK, 2 * HD), lambda h, index: (0, h))
    heads = pl.BlockSpec((CHIP_TOK, WIDE), lambda h, index: (0, h))
    return pl.pallas_call(
        backward_kernel,
        grid_spec=pltpu.PrefetchScalarGridSpec(
            num_scalar_prefetch=1,
            grid=(HEADS,),
            in_specs=[
                pl.BlockSpec((CHIP_TOK, WIDE), lambda h, index: (0, (index[0] % CORES) * HEADS + h)),
                heads,
                kv,
                kv,
            ],
            out_specs=[heads, kv, kv],
            scratch_shapes=[
                pltpu.VMEM((4 * TOK, CORES * WIDE), jnp.bfloat16),
                pltpu.VMEM((4 * TOK, CORES * WIDE), jnp.bfloat16),
            ],
        ),
        out_shape=[
            jax.ShapeDtypeStruct((CHIP_TOK, HALF), jnp.float32),
            jax.ShapeDtypeStruct(before.shape, jnp.bfloat16),
            jax.ShapeDtypeStruct(own.shape, jnp.float32),
        ],
        compiler_params=pltpu.CompilerParams(vmem_limit_bytes=24 * 2**20),
        cost_estimate=pl.CostEstimate(flops=3*10**9, bytes_accessed=10**6, transcendentals=0),
        name="backward_attention",
    )(index, normed, upper, before, own)


def piece_columns(y, pieces):
    firsts, at = [], 0
    block = pieces[0].shape[0]
    for piece in pieces:
        firsts.append(pl.multiple_of(((y + at // block) % Y) * block, block) + at % block)
        at += piece.shape[0]
    return firsts


def project_kernel(y_ref, normed_ref, beside_ref, *refs):
    *pieces, out_ref = refs
    width = pieces[0].shape[1]
    total = jnp.zeros((normed_ref.shape[0], width), jnp.float32)
    for first, piece in zip(piece_columns(y_ref[0], pieces), pieces):
        rows = piece.shape[0]
        part = normed_ref[:, pl.ds(pl.multiple_of(first, rows), rows)]
        total += jnp.dot(part, piece[...], preferred_element_type=jnp.float32)
    rows = total.shape[0]
    out_ref[:rows, :] = total.astype(out_ref.dtype)
    if out_ref.shape[0] > rows:
        out_ref[rows:, :] = beside_ref[...]


SCALARS = pl.BlockSpec(memory_space=pltpu.SMEM)
WHOLE = pl.BlockSpec(memory_space=pltpu.VMEM)


def project(y, normed, pieces, beside, with_beside):
    rows = normed.shape[0] + (beside.shape[0] if with_beside else 0)
    return pl.pallas_call(
        project_kernel,
        in_specs=[SCALARS] + [WHOLE] * (2 + len(pieces)),
        out_specs=WHOLE,
        out_shape=jax.ShapeDtypeStruct((rows, pieces[0].shape[1]), jnp.bfloat16),
        compiler_params=pltpu.CompilerParams(vmem_limit_bytes=16 * 2**20),
        cost_estimate=BRIEF,
        name="project",
    )(y, normed, beside, *pieces)


def partial_kernel(where_ref, own_ref, after_ref, dq_ref, *refs):
    *pieces, out_ref = refs
    core, y = where_ref[1], where_ref[2]
    rows = pl.ds(pl.multiple_of(where_ref[0] * TOK, TOK), TOK)
    grad_kv = (own_ref[rows, :] + after_ref[rows, :].astype(jnp.float32)).astype(jnp.bfloat16)
    for first, piece in zip(piece_columns(y, pieces), pieces):
        count = piece.shape[0]
        grad = lax.dot_general(
            grad_kv, piece[...], (((1,), (1,)), ((), ())), preferred_element_type=jnp.float32
        )
        dq = dq_ref[rows, pl.ds(pl.multiple_of(first % HALF, count), count)]
        grad += jnp.where(first // HALF == core, dq, 0.0)
        out_ref[:, pl.ds(pl.multiple_of(first, count), count)] = grad.astype(out_ref.dtype)


def partial_grad(where, own, after, dq, pieces, kind):
    return pl.pallas_call(
        partial_kernel,
        in_specs=[SCALARS] + [WHOLE] * (3 + len(pieces)),
        out_specs=WHOLE,
        out_shape=jax.ShapeDtypeStruct((TOK, CORES * HALF), kind),
        compiler_params=pltpu.CompilerParams(vmem_limit_bytes=20 * 2**20),
        cost_estimate=BRIEF,
        name="partial_grad",
    )(where, own, after, dq, *pieces)


def input_grad_kernel(
    own_ref, other_ref, x_ref, upper_ref, gain_ref, out_ref, gain_grad_ref, grad_ref
):
    features = x_ref.shape[1]
    width = 512
    blocks = [slice(at, at + width) for at in range(0, features, width)]
    squares = jnp.zeros((TOK, 1), jnp.float32)
    for cols in blocks:
        part = x_ref[:, cols].astype(jnp.float32)
        squares += jnp.sum(part * part, axis=-1, keepdims=True)
    inv_rms = lax.rsqrt(squares / features + EPSILON)
    inner = jnp.zeros((TOK, 1), jnp.float32)
    for cols in blocks:
        grad = own_ref[:, cols] + other_ref[:, cols].astype(jnp.float32)
        scaled = x_ref[:, cols].astype(jnp.float32) * inv_rms
        product = grad * scaled
        gain_grad_ref[:, cols] = jnp.sum(product, axis=0, keepdims=True)
        gain = gain_ref[:, cols]
        inner += jnp.sum(product * gain, axis=-1, keepdims=True)
        grad_ref[:, cols] = grad * gain
    mean = inner * (1.0 / features)
    for cols in blocks:
        scaled = x_ref[:, cols].astype(jnp.float32) * inv_rms
        out = inv_rms * (grad_ref[:, cols] - scaled * mean)
        out_ref[:, cols] = (out + upper_ref[:, cols].astype(jnp.float32)).astype(jnp.bfloat16)


def input_grad(own, other, x, upper, gain_row):
    features = x.shape[1]
    return pl.pallas_call(
        input_grad_kernel,
        in_specs=[WHOLE] * 5,
        out_specs=[WHOLE] * 2,
        out_shape=[
            jax.ShapeDtypeStruct((TOK, features), jnp.bfloat16),
            jax.ShapeDtypeStruct((1, features), jnp.float32),
        ],
        scratch_shapes=[pltpu.VMEM((TOK, features), jnp.float32)],
        compiler_params=pltpu.CompilerParams(vmem_limit_bytes=16 * 2**20),
        cost_estimate=BRIEF,
        name="input_grad",
    )(own, other, x, upper, gain_row)


def in_three(value):
    terms = []
    for _ in range(3):
        term = lax.reduce_precision(value, 8, 7)
        terms.append(term.astype(jnp.bfloat16))
        value = value - term
    return jnp.concatenate(terms, axis=0)


def body(section_in, back_in, upstream, gains, kv_weight):
    index = lax.axis_index("ctx").astype(jnp.int32)
    core, z_lo, y = index % CORES, (index // CORES) % Z_LO, index // (CORES * Z_LO)
    place, y_place = index.reshape(1), y.reshape(1)
    x_back, upper_in = back_in[0], upstream[0]

    chip_x_fwd = chip_rows(section_in[0], swap(section_in[0]), core)
    crossing = columns_of(chip_x_fwd, core)
    run, crossing = lax.optimization_barrier((gather_run(kv_weight[0], core, z_lo), crossing))
    pieces, crossed, first_step = gather_weight(run, crossing)

    later_x, later_upper, _ = lax.optimization_barrier((x_back, upper_in, first_step))
    chip_x_back = chip_rows(x_back, swap(later_x), core)
    chip_back, _ = norm_forward(chip_x_back, gains)
    chip_fwd, inv_fwd = norm_forward(chip_x_fwd, gains)
    chip_upper = chip_columns(later_upper, core)

    width = pieces[0].shape[1]
    norms = jnp.pad(inv_fwd.reshape(1, CHIP_TOK), ((0, 0), (0, width - CHIP_TOK)))
    beside = in_three(jnp.concatenate([columns_of(gains, core).reshape(-1, width), norms], axis=0))
    beside = jnp.pad(beside, ((0, 16 - beside.shape[0]), (0, 0)))
    chip_back, chip_fwd, chip_upper, beside = lax.optimization_barrier(
        (chip_back, chip_fwd, chip_upper, beside)
    )

    kv_back = project(y_place, chip_back, pieces, beside, False)
    kv_back, chip_fwd = lax.optimization_barrier((kv_back, chip_fwd))
    before = to_next_chip(kv_back)
    kv_half = halfway(project(y_place, chip_fwd, pieces, beside, True))

    dq, grad_before, grad_own = backward_attention(place, chip_back, chip_upper, before, kv_back)
    kv_half, after, crossed = lax.optimization_barrier(
        (kv_half, to_chip_before(grad_before), crossed)
    )
    kv_here = arrive(kv_half, 1)

    def partial(row, kind):
        return partial_grad(jnp.stack([row, core, y]), grad_own, after, dq, pieces, kind)

    away = swap(partial(1 - core, jnp.bfloat16))
    home = partial(core, jnp.float32)
    away, home, kv_here = lax.optimization_barrier((away, home, kv_here))
    grad_in, gain_grad = input_grad(home, away, x_back, upper_in, gains)
    half_sent = halfway(grad_in)

    kv_here, _ = lax.optimization_barrier((kv_here, grad_in))
    before_here = to_next_chip(kv_here)
    gain_grad = gain_grad + swap(gain_grad)
    for bit in (1, 2, 4):
        gain_grad = gain_grad + over_ctx(gain_grad, lambda y, z, c: (y ^ bit, z, c))
    half_sent, gain_grad, crossed = lax.optimization_barrier((half_sent, gain_grad, crossed))
    next_grad = arrive(half_sent, -1)
    gain_grad = gain_grad + over_ctx(gain_grad, lambda y, z, c: (y, z ^ 1, c))
    next_grad, gain_grad = lax.optimization_barrier((next_grad, gain_grad))
    gain_grad = gain_grad + over_ctx(gain_grad, lambda y, z, c: (y, z ^ 2, c))

    out = forward_attention(place, crossed, before_here, kv_here)
    first, second = out[:TOK], out[TOK:]
    mine = jnp.where(core == 0, first, second)
    other = swap(jnp.where(core == 0, second, first))
    next_in = jnp.concatenate(
        [jnp.where(core == 0, mine, other), jnp.where(core == 0, other, mine)], axis=1
    )
    return (next_in[None], next_grad[None], gain_grad)


def solution(mesh):
    in_specs = (
        P("section", "ctx", None),
        P("section", "ctx", None),
        P("section", "ctx", None),
        P("section", None),
        P("section", "ctx", None),
    )
    out_specs = (P("section", "ctx", None), P("section", "ctx", None), P("section", None))
    return jax.shard_map(body, mesh=mesh, in_specs=in_specs, out_specs=out_specs, check_vma=False)
```

```python
import functools

import jax
import jax.numpy as jnp
from jax import lax
from jax.experimental import pallas as pl
from jax.experimental.pallas import tpu as pltpu
from jax.sharding import PartitionSpec as P

HD = 128
STEPS = 2
EPSILON = 1e-05
GROUP = 8
KVH = 4
TOK = 128
SPAN = (STEPS + 1) * TOK

X, Z_HI, Y, Z_LO, CORES = 4, 2, 8, 4, 2
Z = Z_HI * Z_LO
CHIPS = Y * Z_LO
CTX = Y * Z_LO * CORES

HEADS = KVH // CORES
CHIP_TOK = CORES * TOK
HALF = HEADS * GROUP * HD

SCALE = HD ** (-0.5)
LOG2E = 1.4426950408889634


def ctx_pairs(move):
    pairs = []
    for c in range(CTX):
        target = move(c // (Z_LO * CORES), (c // CORES) % Z_LO, c % CORES)
        if target is not None:
            y, z_lo, core = target
            pairs.append((c, (y * Z_LO + z_lo) * CORES + core))
    return pairs


def over_ctx(value, move):
    return lax.ppermute(value, "ctx", ctx_pairs(move))


def grid_pairs(move):
    pairs = []
    for x in range(X):
        for z in range(Z):
            for core in range(CORES):
                new_x, new_z = move(x, z, core)
                new_x, new_z = (new_x % X, new_z % Z)
                for y in range(Y):
                    source = (x * Z_HI + z // Z_LO) * CTX + (y * Z_LO + z % Z_LO) * CORES + core
                    target = (new_x * Z_HI + new_z // Z_LO) * CTX + (y * Z_LO + new_z % Z_LO) * CORES + core
                    pairs.append((source, target))
    return pairs


def over_grid(value, move):
    return lax.ppermute(value, ("section", "ctx"), grid_pairs(move))


WAY = (2, -2)


def halfway(value):
    return over_grid(value, lambda x, z, core: (x, z + WAY[core]))


def arrive(value, distance):
    def move(x, z, core):
        z_hi = ((z - WAY[core]) % Z) // Z_LO
        cross = (1 if z_hi == Z_HI - 1 else 0) if distance == 1 else (-1 if z_hi == 0 else 0)
        return (x + cross, z + WAY[core])

    return over_grid(value, move)


def norm_forward(section_x, gain_row):
    values = section_x.astype(jnp.float32)
    inv_rms = lax.rsqrt(jnp.mean(values * values, axis=-1, keepdims=True) + EPSILON)
    return (values * inv_rms * gain_row).astype(jnp.bfloat16), inv_rms


def by_head(kv_columns):
    parts = []
    for head in range(KVH):
        parts.append(kv_columns[:, head * HD : (head + 1) * HD])
        parts.append(kv_columns[:, (KVH + head) * HD : (KVH + head + 1) * HD])
    return jnp.concatenate(parts, axis=1)


def gather_run(own_rows, core, z_lo):
    half = own_rows.shape[1] // 2
    columns = by_head(own_rows)
    low, high = columns[:, :half], columns[:, half:]
    keep = jnp.where(core == 0, low, high)
    received = swap(jnp.where(core == 0, high, low))
    chip = chip_rows(keep, received, core)
    rows = chip.shape[0]
    pieces = [chip]
    for step in range(1, Z_LO):
        pieces.append(over_ctx(chip, lambda y, z, c, step=step: (y, (z + step) % Z_LO, c)))
    back = pieces[::-1]
    return lax.dynamic_slice_in_dim(
        jnp.concatenate(back + back[:-1], axis=0), (Z_LO - 1 - z_lo) * rows, Z_LO * rows, 0
    )


def gather_weight(run, crossing):
    def up(piece):
        return over_ctx(piece, lambda y, z, c: ((y + 1) % Y, z, c))

    def down(piece):
        return over_ctx(piece, lambda y, z, c: ((y - 1) % Y, z, c))

    crossing = halfway(crossing)
    rising, falling = [up(run)], [down(run)]
    rising.append(up(rising[0]))
    falling.append(down(falling[0]))
    rising[1], falling[1], crossing = lax.optimization_barrier((rising[1], falling[1], crossing))
    rising.append(up(rising[1]))
    falling.append(down(falling[1]))
    middle = run.shape[0] // 2
    rising.append(up(rising[2][:middle]))
    falling.append(down(falling[2][middle:]))
    pieces = [run, *falling[:3], rising[3], falling[3], *rising[:3][::-1]]
    return pieces, arrive(crossing, 1), rising[0]


def swap(value):
    return over_ctx(value, lambda y, z, c: (y, z, 1 - c))


def chip_rows(own, partner, core):
    return jnp.concatenate(
        [jnp.where(core == 0, own, partner), jnp.where(core == 0, partner, own)], axis=0
    )


def to_next_chip(value):
    pairs = [(i, i + CORES) for i in range(CTX - CORES)]
    return lax.ppermute(value, "ctx", pairs)


def to_chip_before(value):
    pairs = [(i, i - CORES) for i in range(CORES, CTX)]
    return lax.ppermute(value, "ctx", pairs)


def columns_of(value, core):
    return lax.dynamic_slice_in_dim(value, core * HALF, HALF, 1)


def chip_columns(value, core):
    return chip_rows(columns_of(value, core), swap(columns_of(value, 1 - core)), core)


def stacked(ref, tokens):
    rows = slice(tokens * TOK, (tokens + 1) * TOK)
    return jnp.concatenate([ref[rows, g * HD : (g + 1) * HD] for g in range(GROUP)], axis=0)


def masked_scores(keys, queries, tokens, any_before):
    scores = lax.dot_general(
        keys, queries, (((1,), (1,)), ((), ())), preferred_element_type=jnp.float32
    )
    across = queries.shape[0]
    before = (STEPS - tokens) * TOK
    seen = lax.broadcasted_iota(jnp.int32, (TOK, across), 0)
    query = lax.broadcasted_iota(jnp.int32, (TOK, across), 1) % TOK
    parts = [jnp.where(any_before, scores[:before], -1e30)]
    if tokens:
        parts.append(scores[before : STEPS * TOK])
    parts.append(jnp.where(seen <= query, scores[STEPS * TOK :], -1e30))
    return jnp.concatenate(parts, axis=0)


PAIR = 2
WIDE = GROUP * HD

BESIDE = HALF // (2 * HEADS * HD) + 1

BRIEF = pl.CostEstimate(flops=1000, bytes_accessed=1000, transcendentals=0)


def forward_kernel(index_ref, x_ref, beside_ref, before_ref, own_ref, out_ref):
    any_before = index_ref[0] >= CORES
    beside = beside_ref[...].astype(jnp.float32)
    beside = beside[:BESIDE] + beside[BESIDE : 2 * BESIDE] + beside[2 * BESIDE : 3 * BESIDE]
    per_head = WIDE // beside.shape[1]
    head = pl.program_id(0)
    gain_rows = jnp.where(head == 0, beside[:per_head], beside[per_head : 2 * per_head])
    gain = jnp.concatenate([gain_rows[i : i + 1] for i in range(per_head)], axis=1)
    inv_row = beside[2 * per_head : 2 * per_head + 1, :CHIP_TOK]
    inv_rms = jnp.broadcast_to(inv_row, (HD, CHIP_TOK)).T
    keys = jnp.concatenate([before_ref[:, :HD], own_ref[:, :HD]], axis=0)
    values = jnp.concatenate([before_ref[:, HD:], own_ref[:, HD:]], axis=0)
    values_t = values.astype(jnp.float32).T.astype(jnp.bfloat16)
    for tokens in range(CORES):
        span = slice(tokens * TOK, tokens * TOK + SPAN)
        rows = slice(tokens * TOK, (tokens + 1) * TOK)
        inv = inv_rms[rows]
        for pair in range(GROUP // PAIR):
            cols = [
                slice(g * HD, (g + 1) * HD) for g in range(pair * PAIR, (pair + 1) * PAIR)
            ]
            x = [x_ref[rows, at].astype(jnp.float32) for at in cols]
            queries = jnp.concatenate(
                [(part * inv * gain[:, at]).astype(jnp.bfloat16) for part, at in zip(x, cols)],
                axis=0,
            )
            scores = masked_scores(keys[span], queries, tokens, any_before)
            top = jnp.max(scores, axis=0, keepdims=True)
            terms = jnp.exp2((scores - top) * (SCALE * LOG2E))
            total = jnp.sum(terms, axis=0, keepdims=True)
            attended = jnp.dot(
                values_t[:, span], terms.astype(jnp.bfloat16), preferred_element_type=jnp.float32
            ) * (1.0 / total)
            for g, at in enumerate(cols):
                out = attended[:, g * TOK : (g + 1) * TOK].T + x[g]
                out_ref[rows, at] = out.astype(jnp.bfloat16)


def forward_attention(index, crossed, before, own):
    heads = pl.BlockSpec((CHIP_TOK, WIDE), lambda h, index: (0, h))
    kv = pl.BlockSpec((CHIP_TOK, 2 * HD), lambda h, index: (0, h))
    return pl.pallas_call(
        forward_kernel,
        grid_spec=pltpu.PrefetchScalarGridSpec(
            num_scalar_prefetch=1,
            grid=(HEADS,),
            in_specs=[
                heads,
                pl.BlockSpec((16, own.shape[1]), lambda h, index: (CHIP_TOK // 16, 0)),
                kv,
                kv,
            ],
            out_specs=heads,
        ),
        out_shape=jax.ShapeDtypeStruct((CHIP_TOK, HALF), jnp.bfloat16),
        compiler_params=pltpu.CompilerParams(vmem_limit_bytes=20 * 2**20),
        cost_estimate=BRIEF,
        name="forward_attention",
    )(index, crossed, own, before, own)


def backward_kernel(
    index_ref, normed_ref, upper_ref, before_ref, own_ref, dq_ref, grad_before_ref, grad_own_ref,
    probs_ref, dlog_ref,
):
    any_before = index_ref[0] >= CORES
    keys = jnp.concatenate([before_ref[:, :HD], own_ref[:, :HD]], axis=0)
    values = jnp.concatenate([before_ref[:, HD:], own_ref[:, HD:]], axis=0)
    keys_t = keys.astype(jnp.float32).T.astype(jnp.bfloat16)
    queries = [stacked(normed_ref, tokens) for tokens in range(CORES)]
    uppers = [stacked(upper_ref, tokens) for tokens in range(CORES)]
    for tokens in range(CORES):
        span = slice(tokens * TOK, tokens * TOK + SPAN)
        for pair in range(GROUP // PAIR):
            these = slice(pair * PAIR * TOK, (pair + 1) * PAIR * TOK)
            scores = masked_scores(keys[span], queries[tokens][these], tokens, any_before)
            grad_probs = lax.dot_general(
                values[span],
                uppers[tokens][these],
                (((1,), (1,)), ((), ())),
                preferred_element_type=jnp.float32,
            )
            top = jnp.max(scores, axis=0, keepdims=True)
            terms = jnp.exp2((scores - top) * (SCALE * LOG2E))
            inverse = 1.0 / jnp.sum(terms, axis=0, keepdims=True)
            row_dot = jnp.sum(terms * grad_probs, axis=0, keepdims=True) * inverse
            probs = terms * inverse
            cols = slice(tokens * WIDE + these.start, tokens * WIDE + these.stop)
            probs_ref[span, cols] = probs.astype(jnp.bfloat16)
            dlog_ref[span, cols] = (probs * ((grad_probs - row_dot) * SCALE)).astype(jnp.bfloat16)
        dlogits = dlog_ref[span, tokens * WIDE : (tokens + 1) * WIDE]
        grad_query = jnp.dot(keys_t[:, span], dlogits, preferred_element_type=jnp.float32)
        rows = slice(tokens * TOK, (tokens + 1) * TOK)
        for g in range(GROUP):
            dq_ref[rows, g * HD : (g + 1) * HD] = grad_query[:, g * TOK : (g + 1) * TOK].T
    for left, factors, first in ((dlog_ref, queries, 0), (probs_ref, uppers, HD)):
        cols = slice(first, first + HD)

        def product(rows, tokens, last):
            factor = jnp.concatenate(factors[tokens:last], axis=0)
            return jnp.dot(
                left[rows, tokens * WIDE : last * WIDE], factor, preferred_element_type=jnp.float32
            )

        middle = product(slice(TOK, 3 * TOK), 0, 2)
        grad_before_ref[:TOK, cols] = product(slice(0, TOK), 0, 1).astype(jnp.bfloat16)
        grad_before_ref[TOK:, cols] = middle[:TOK].astype(jnp.bfloat16)
        grad_own_ref[:TOK, cols] = middle[TOK:]
        grad_own_ref[TOK:, cols] = product(slice(3 * TOK, 4 * TOK), 1, 2)


def backward_attention(index, normed, upper, before, own):
    kv = pl.BlockSpec((CHIP_TOK, 2 * HD), lambda h, index: (0, h))
    heads = pl.BlockSpec((CHIP_TOK, WIDE), lambda h, index: (0, h))
    return pl.pallas_call(
        backward_kernel,
        grid_spec=pltpu.PrefetchScalarGridSpec(
            num_scalar_prefetch=1,
            grid=(HEADS,),
            in_specs=[
                pl.BlockSpec((CHIP_TOK, WIDE), lambda h, index: (0, (index[0] % CORES) * HEADS + h)),
                heads,
                kv,
                kv,
            ],
            out_specs=[heads, kv, kv],
            scratch_shapes=[
                pltpu.VMEM((4 * TOK, CORES * WIDE), jnp.bfloat16),
                pltpu.VMEM((4 * TOK, CORES * WIDE), jnp.bfloat16),
            ],
        ),
        out_shape=[
            jax.ShapeDtypeStruct((CHIP_TOK, HALF), jnp.float32),
            jax.ShapeDtypeStruct(before.shape, jnp.bfloat16),
            jax.ShapeDtypeStruct(own.shape, jnp.float32),
        ],
        compiler_params=pltpu.CompilerParams(vmem_limit_bytes=24 * 2**20),
        cost_estimate=BRIEF,
        name="backward_attention",
    )(index, normed, upper, before, own)


def piece_columns(y, pieces):
    firsts, at = [], 0
    block = pieces[0].shape[0]
    for piece in pieces:
        firsts.append(pl.multiple_of(((y + at // block) % Y) * block, block) + at % block)
        at += piece.shape[0]
    return firsts


def project_kernel(y_ref, normed_ref, beside_ref, *refs):
    *pieces, out_ref = refs
    width = pieces[0].shape[1]
    total = jnp.zeros((normed_ref.shape[0], width), jnp.float32)
    for first, piece in zip(piece_columns(y_ref[0], pieces), pieces):
        rows = piece.shape[0]
        part = normed_ref[:, pl.ds(pl.multiple_of(first, rows), rows)]
        total += jnp.dot(part, piece[...], preferred_element_type=jnp.float32)
    rows = total.shape[0]
    out_ref[:rows, :] = total.astype(out_ref.dtype)
    if out_ref.shape[0] > rows:
        out_ref[rows:, :] = beside_ref[...]


SCALARS = pl.BlockSpec(memory_space=pltpu.SMEM)
WHOLE = pl.BlockSpec(memory_space=pltpu.VMEM)


def project(y, normed, pieces, beside, with_beside):
    rows = normed.shape[0] + (beside.shape[0] if with_beside else 0)
    return pl.pallas_call(
        project_kernel,
        in_specs=[SCALARS] + [WHOLE] * (2 + len(pieces)),
        out_specs=WHOLE,
        out_shape=jax.ShapeDtypeStruct((rows, pieces[0].shape[1]), jnp.bfloat16),
        compiler_params=pltpu.CompilerParams(vmem_limit_bytes=16 * 2**20),
        cost_estimate=BRIEF,
        name="project",
    )(y, normed, beside, *pieces)


def partial_kernel(where_ref, own_ref, after_ref, dq_ref, *refs):
    *pieces, out_ref = refs
    core, y = where_ref[1], where_ref[2]
    rows = pl.ds(pl.multiple_of(where_ref[0] * TOK, TOK), TOK)
    grad_kv = (own_ref[rows, :] + after_ref[rows, :].astype(jnp.float32)).astype(jnp.bfloat16)
    for first, piece in zip(piece_columns(y, pieces), pieces):
        count = piece.shape[0]
        grad = lax.dot_general(
            grad_kv, piece[...], (((1,), (1,)), ((), ())), preferred_element_type=jnp.float32
        )
        dq = dq_ref[rows, pl.ds(pl.multiple_of(first % HALF, count), count)]
        grad += jnp.where(first // HALF == core, dq, 0.0)
        out_ref[:, pl.ds(pl.multiple_of(first, count), count)] = grad.astype(out_ref.dtype)


def partial_grad(where, own, after, dq, pieces, kind):
    return pl.pallas_call(
        partial_kernel,
        in_specs=[SCALARS] + [WHOLE] * (3 + len(pieces)),
        out_specs=WHOLE,
        out_shape=jax.ShapeDtypeStruct((TOK, CORES * HALF), kind),
        compiler_params=pltpu.CompilerParams(vmem_limit_bytes=20 * 2**20),
        cost_estimate=BRIEF,
        name="partial_grad",
    )(where, own, after, dq, *pieces)


def input_grad_kernel(
    own_ref, other_ref, x_ref, upper_ref, gain_ref, out_ref, gain_grad_ref, grad_ref
):
    features = x_ref.shape[1]
    width = 512
    blocks = [slice(at, at + width) for at in range(0, features, width)]
    squares = jnp.zeros((TOK, 1), jnp.float32)
    for cols in blocks:
        part = x_ref[:, cols].astype(jnp.float32)
        squares += jnp.sum(part * part, axis=-1, keepdims=True)
    inv_rms = lax.rsqrt(squares / features + EPSILON)
    inner = jnp.zeros((TOK, 1), jnp.float32)
    for cols in blocks:
        grad = own_ref[:, cols] + other_ref[:, cols].astype(jnp.float32)
        scaled = x_ref[:, cols].astype(jnp.float32) * inv_rms
        product = grad * scaled
        gain_grad_ref[:, cols] = jnp.sum(product, axis=0, keepdims=True)
        gain = gain_ref[:, cols]
        inner += jnp.sum(product * gain, axis=-1, keepdims=True)
        grad_ref[:, cols] = grad * gain
    mean = inner * (1.0 / features)
    for cols in blocks:
        scaled = x_ref[:, cols].astype(jnp.float32) * inv_rms
        out = inv_rms * (grad_ref[:, cols] - scaled * mean)
        out_ref[:, cols] = (out + upper_ref[:, cols].astype(jnp.float32)).astype(jnp.bfloat16)


def input_grad(own, other, x, upper, gain_row):
    features = x.shape[1]
    return pl.pallas_call(
        input_grad_kernel,
        in_specs=[WHOLE] * 5,
        out_specs=[WHOLE] * 2,
        out_shape=[
            jax.ShapeDtypeStruct((TOK, features), jnp.bfloat16),
            jax.ShapeDtypeStruct((1, features), jnp.float32),
        ],
        scratch_shapes=[pltpu.VMEM((TOK, features), jnp.float32)],
        compiler_params=pltpu.CompilerParams(vmem_limit_bytes=16 * 2**20),
        cost_estimate=BRIEF,
        name="input_grad",
    )(own, other, x, upper, gain_row)


def in_three(value):
    terms = []
    for _ in range(3):
        term = lax.reduce_precision(value, 8, 7)
        terms.append(term.astype(jnp.bfloat16))
        value = value - term
    return jnp.concatenate(terms, axis=0)


def body(section_in, back_in, upstream, gains, kv_weight):
    index = lax.axis_index("ctx").astype(jnp.int32)
    core, z_lo, y = index % CORES, (index // CORES) % Z_LO, index // (CORES * Z_LO)
    place, y_place = index.reshape(1), y.reshape(1)
    x_back, upper_in = back_in[0], upstream[0]

    chip_x_fwd = chip_rows(section_in[0], swap(section_in[0]), core)
    crossing = columns_of(chip_x_fwd, core)
    run, crossing = lax.optimization_barrier((gather_run(kv_weight[0], core, z_lo), crossing))
    pieces, crossed, first_step = gather_weight(run, crossing)

    later_x, later_upper, _ = lax.optimization_barrier((x_back, upper_in, first_step))
    chip_x_back = chip_rows(x_back, swap(later_x), core)
    chip_back, _ = norm_forward(chip_x_back, gains)
    chip_fwd, inv_fwd = norm_forward(chip_x_fwd, gains)
    chip_upper = chip_columns(later_upper, core)

    width = pieces[0].shape[1]
    norms = jnp.pad(inv_fwd.reshape(1, CHIP_TOK), ((0, 0), (0, width - CHIP_TOK)))
    beside = in_three(jnp.concatenate([columns_of(gains, core).reshape(-1, width), norms], axis=0))
    beside = jnp.pad(beside, ((0, 16 - beside.shape[0]), (0, 0)))
    chip_back, chip_fwd, chip_upper, beside = lax.optimization_barrier(
        (chip_back, chip_fwd, chip_upper, beside)
    )

    kv_back = project(y_place, chip_back, pieces, beside, False)
    kv_back, chip_fwd = lax.optimization_barrier((kv_back, chip_fwd))
    before = to_next_chip(kv_back)
    kv_half = halfway(project(y_place, chip_fwd, pieces, beside, True))

    dq, grad_before, grad_own = backward_attention(place, chip_back, chip_upper, before, kv_back)
    kv_half, after, crossed = lax.optimization_barrier(
        (kv_half, to_chip_before(grad_before), crossed)
    )

    def partial(row, kind):
        return partial_grad(jnp.stack([row, core, y]), grad_own, after, dq, pieces, kind)

    away = swap(partial(1 - core, jnp.bfloat16))
    home = partial(core, jnp.float32)
    grad_in, gain_grad = input_grad(home, away, x_back, upper_in, gains)
    half_sent = halfway(grad_in)

    kv_half, _ = lax.optimization_barrier((kv_half, grad_in))
    kv_here = arrive(kv_half, 1)
    before_here = to_next_chip(kv_here)
    gain_grad = gain_grad + swap(gain_grad)
    for bit in (1, 2):
        gain_grad = gain_grad + over_ctx(gain_grad, lambda y, z, c: (y ^ bit, z, c))
    half_sent, gain_grad, crossed = lax.optimization_barrier((half_sent, gain_grad, crossed))
    next_grad = arrive(half_sent, -1)
    gain_grad = gain_grad + over_ctx(gain_grad, lambda y, z, c: (y ^ 4, z, c))
    gain_grad = gain_grad + over_ctx(gain_grad, lambda y, z, c: (y, z ^ 1, c))
    next_grad, gain_grad = lax.optimization_barrier((next_grad, gain_grad))
    gain_grad = gain_grad + over_ctx(gain_grad, lambda y, z, c: (y, z ^ 2, c))

    out = forward_attention(place, crossed, before_here, kv_here)
    first, second = out[:TOK], out[TOK:]
    mine = jnp.where(core == 0, first, second)
    other = swap(jnp.where(core == 0, second, first))
    next_in = jnp.concatenate(
        [jnp.where(core == 0, mine, other), jnp.where(core == 0, other, mine)], axis=1
    )
    return (next_in[None], next_grad[None], gain_grad)


def solution(mesh):
    in_specs = (
        P("section", "ctx", None),
        P("section", "ctx", None),
        P("section", "ctx", None),
        P("section", None),
        P("section", "ctx", None),
    )
    out_specs = (P("section", "ctx", None), P("section", "ctx", None), P("section", None))
    return jax.shard_map(body, mesh=mesh, in_specs=in_specs, out_specs=out_specs, check_vma=False)
```
